256 devices in a mesh: layer: 4 (over x), latent: 64 (over y, z, core).
Axes of the slice: x: 4, y: 4, z: 8, core: 2. Of those that a mesh axis runs over, the one named last changes fastest.
Arguments:
- residual: bfloat16 [4, 512, 1792], P('layer', 'latent'), may hold values from -6 to 6
- target: bfloat16 [4, 512, 1792], P('layer', 'latent'), may hold values from -6 to 6
- enc_weight: bfloat16 [4, 1792, 16384], P('layer', None, 'latent'), may hold values from -0.125 to 0.125
- enc_bias: float32 [4, 16384], P('layer', 'latent'), may hold values from -3 to 3
- dec_weight: bfloat16 [4, 4, 16384, 1792], P(None, 'layer', 'latent'), may hold values from -0.0625 to 0.0625
- active: int32 [4, 8, 32], replicated, may hold values from 0 to 63, all different within a row; in each aligned block of 8 rows (0 to 7, 8 to 15, ..., all dimensions but the last counted through in order) at most 6 rows name the same one
Outputs:
- loss: float32 [], replicated
- enc_grad: bfloat16 [4, 1792, 16384], P('layer', None, 'latent')
- bias_grad: float32 [4, 16384], P('layer', 'latent')
- dec_grad: bfloat16 [4, 4, 16384, 1792], P(None, 'layer', 'latent')
The draws below stay inside these ranges and needn't reach their ends.
Inputs may be any that keep to these rules, and one draw needn't show every extreme that they name: `active`: each row lists 32 different blocks of its layer; within one layer no block is listed on more than 6 token tiles, and in every draw some block of some layer is listed on exactly 6.
All inputs are finite; a program needn't handle non-finite values.
Results may differ from the reference program's by a relative error of at most 0.023.
Values may be sent and summed in bfloat16 or wider, within the bound.
No kernel may reach another device: no remote copies, remote signals or barrier semaphores. Data moves between devices by JAX's collectives and lax.ppermute only.
A program may use at most 128 MiB of HBM per device.

```python
import math
import jax
import jax.numpy as jnp
import numpy as np
from jax import lax

D = 1792
BLOCK = 256
TILE = 64
NTILE = 8
LAYERS = 4
FEATS = 16384
BLOCKS = 64
ACT = 32
CAP = 6
TOKENS = 512


def block_scale(stream_key, shape, split, least, largest):
    loudness = 1.0
    for dim, shards_of in split:
        heights = jax.random.uniform(jax.random.fold_in(jax.random.fold_in(stream_key, 6), dim), (shards_of,), jnp.float32, least / len(split), largest / len(split))
        loudness = loudness * jnp.repeat(jnp.exp(heights), shape[dim] // shards_of).reshape((-1,) + (1,) * (len(shape) - 1 - dim))
    return loudness


def shared_out(stream_key, own, number, rows, count, top, limit, skew):
    sequence = jax.random.permutation(stream_key, count)
    heavy_load, usual = shares(count, rows * top, limit, skew, True), shares(count, rows * top, limit, skew, False)
    places = jnp.arange(count)

    def named(sizes, rotation):
        used = int((sizes > 0).sum())
        fixed = max(1, used // 4)
        passed = fixed + (places - fixed + rotation * (used - fixed)) % max(1, count - fixed)
        return jnp.zeros((count,), jnp.int32).at[sequence[jnp.where(places < fixed, places, passed)]].set(jnp.asarray(sizes, jnp.int32))

    sizes = jnp.where(number % 4 == 0, named(heavy_load, number // 4), named(usual, number - number // 4 - 1))
    mixed = jax.random.permutation(jax.random.fold_in(own, 3), count)
    donor, taker = mixed[0:count // 2 * 2:2], mixed[1:count // 2 * 2:2]
    margin = jnp.minimum(sizes[donor] - 1, limit - sizes[taker]) // 2
    margin = jnp.where((donor == sequence[0]) | (taker == sequence[0]) | (sizes[taker] == 0), 0, jnp.maximum(margin, 0))
    passed = jax.random.randint(jax.random.fold_in(own, 4), (count // 2,), 0, 1 << 20) % (margin + 1)
    sizes = sizes.at[donor].add(-passed).at[taker].add(passed)
    labels = jnp.searchsorted(jnp.cumsum(sizes), jnp.arange(rows * top), side="right").astype(jnp.int32)
    grid = labels.reshape(top, rows).T
    grid = grid[jax.random.permutation(jax.random.fold_in(own, 1), rows)]
    rotation = jax.random.randint(jax.random.fold_in(own, 2), (rows, 1), 0, top)
    return jnp.take_along_axis(grid, (jnp.arange(top)[None, :] + rotation) % top, axis=1)


def shares(number_of, total, reach, skew, full):
    portions = [(1 << 20) // math.isqrt(grade ** skew) + 1 for grade in range(1, number_of + 1)]
    largest = reach if full else min(reach, max(-(-total // number_of), total * portions[0] // sum(portions)))
    least = 1 if total - largest >= number_of - 1 else 0
    holding, spare = [largest] + [least] * (number_of - 1), total - largest - least * (number_of - 1)
    while spare > 0:
        free = [i for i in range(1, number_of) if holding[i] < largest] or [i for i in range(1, number_of) if holding[i] < reach]
        pool, budget = sum([portions[i] for i in free]), spare
        for i in free:
            extra = min(reach - holding[i], max(1, budget * portions[i] // pool), spare)
            holding[i] = holding[i] + extra
            spare = spare - extra
    return np.array(holding)


def bell_draw(stream_key, shape, deviation, bound, cuts=(), held_as=jnp.bfloat16):
    drawn = jax.random.normal(stream_key, shape, jnp.float32) * deviation
    if len(cuts) > 0:
        drawn = block_scale(stream_key, shape, cuts, -0.22, 0.18) * drawn
    return jnp.clip(drawn, min=-bound, max=bound).astype(held_as)


def setup_inputs(seed: int = 0) -> dict:
    key_list = jax.random.split(jax.random.key(seed), 7)
    residual = bell_draw(key_list[0], (LAYERS, TOKENS, D), 1.0, 6.0, ((0, 4), (1, 64)))
    target = bell_draw(key_list[1], (LAYERS, TOKENS, D), 1.0, 6.0, ((0, 4), (1, 64)))
    enc_weight = bell_draw(key_list[2], (LAYERS, D, FEATS), D ** -0.5, 0.125, ((0, 4), (2, 64)))
    enc_bias = bell_draw(key_list[3], (LAYERS, FEATS), 0.5, 3.0, ((0, 4), (1, 64)), jnp.float32)
    dec_weight = bell_draw(key_list[4], (LAYERS, LAYERS, FEATS, D), (ACT * BLOCK) ** -0.5, 0.0625, ((1, 4), (2, 64)))
    active_keys = jax.random.split(jax.random.fold_in(key_list[5], 1), LAYERS * NTILE // NTILE)
    active_turns = jax.random.permutation(jax.random.fold_in(key_list[5], 3), LAYERS * NTILE // NTILE)
    active = jax.vmap(lambda own, number: shared_out(jax.random.fold_in(key_list[5], 2), own, number, NTILE, BLOCKS, ACT, CAP, 2))(active_keys, active_turns).reshape((LAYERS, NTILE, ACT))
    return {"residual": residual, "target": target, "enc_weight": enc_weight, "enc_bias": enc_bias, "dec_weight": dec_weight, "active": active}


def reference(residual, target, enc_weight, enc_bias, dec_weight, active):
    layers = residual.shape[0]
    width = ACT * BLOCK
    x_tiles = residual.reshape(layers, NTILE, TILE, D)
    goal = target.reshape(layers, NTILE, TILE, D).astype(jnp.float32)
    enc_blocks = enc_weight.reshape(layers, D, BLOCKS, BLOCK)
    bias_blocks = enc_bias.reshape(layers, BLOCKS, BLOCK)
    dec_blocks = dec_weight.reshape(layers, layers, BLOCKS, BLOCK, D)
    preacts = []
    codes = []
    for source in range(layers):
        def encode(inputs, source=source):
            rows, block_ids = inputs
            weight = jnp.take(enc_blocks[source], block_ids, axis=1).reshape(D, width)
            offset = jnp.take(bias_blocks[source], block_ids, axis=0).reshape(width)
            return jnp.dot(rows, weight, preferred_element_type=jnp.float32) + offset
        preact = lax.map(encode, (x_tiles[source], active[source]))
        preacts.append(preact)
        codes.append(jnp.maximum(preact, 0.0).astype(jnp.bfloat16))
    codes_all = jnp.stack(codes)

    def decode(tile):
        outputs = []
        for dest in range(layers):
            total = jnp.zeros((TILE, D), jnp.float32)
            for source in range(dest + 1):
                weight = jnp.take(dec_blocks[source, dest], active[source, tile], axis=0).reshape(width, D)
                total = total + jnp.dot(codes_all[source, tile], weight, preferred_element_type=jnp.float32)
            outputs.append(total)
        return jnp.stack(outputs)

    recon = lax.map(decode, jnp.arange(NTILE, dtype=jnp.int32))
    errors = jnp.transpose(recon, (1, 0, 2, 3)) - goal
    loss = 0.5 * jnp.mean(errors * errors)
    error_bf = errors.astype(jnp.bfloat16)

    dec_rows = []
    for source in range(layers):
        row = []
        for dest in range(layers):
            if dest < source:
                row.append(jnp.zeros((FEATS, D), jnp.bfloat16))
            else:
                def add_tile(carry, tile, source=source, dest=dest):
                    block_ids = active[source, tile]
                    term = lax.dot_general(codes_all[source, tile], error_bf[dest, tile], (((0,), (0,)), ((), ())), preferred_element_type=jnp.float32)
                    return carry.at[block_ids].add(term.reshape(ACT, BLOCK, D)), None
                carry, _ = lax.scan(add_tile, jnp.zeros((BLOCKS, BLOCK, D), jnp.float32), jnp.arange(NTILE, dtype=jnp.int32))
                row.append((carry / TILE).reshape(FEATS, D).astype(jnp.bfloat16))
        dec_rows.append(jnp.stack(row))
    dec_grad = jnp.stack(dec_rows)

    enc_grads = []
    bias_grads = []
    for source in range(layers):
        def back_tile(carry, tile, source=source):
            enc_sum, bias_sum = carry
            block_ids = active[source, tile]
            code_grad = jnp.zeros((TILE, width), jnp.float32)
            for dest in range(source, layers):
                weight = jnp.take(dec_blocks[source, dest], block_ids, axis=0).reshape(width, D)
                code_grad = code_grad + lax.dot_general(error_bf[dest, tile], weight, (((1,), (1,)), ((), ())), preferred_element_type=jnp.float32)
            pre_grad = jnp.where(preacts[source][tile] > 0, code_grad, jnp.zeros_like(code_grad))
            pre_bf = pre_grad.astype(jnp.bfloat16)
            enc_term = lax.dot_general(x_tiles[source, tile], pre_bf, (((0,), (0,)), ((), ())), preferred_element_type=jnp.float32)
            enc_sum = enc_sum.at[:, block_ids].add(enc_term.reshape(D, ACT, BLOCK))
            bias_sum = bias_sum.at[block_ids].add(jnp.sum(pre_grad, axis=0).reshape(ACT, BLOCK))
            return (enc_sum, bias_sum), None
        start = (jnp.zeros((D, BLOCKS, BLOCK), jnp.float32), jnp.zeros((BLOCKS, BLOCK), jnp.float32))
        (enc_sum, bias_sum), _ = lax.scan(back_tile, start, jnp.arange(NTILE, dtype=jnp.int32))
        enc_grads.append((enc_sum / TILE).reshape(D, FEATS).astype(jnp.bfloat16))
        bias_grads.append((bias_sum / TILE).reshape(FEATS))
    return loss, jnp.stack(enc_grads), jnp.stack(bias_grads), dec_grad
```

```python
import jax
import jax.numpy as jnp
from jax import lax
from jax.sharding import PartitionSpec as P

TILE = 64
NTILE = 8
Y, Z, C = 4, 8, 2
BF = jnp.bfloat16
F32 = jnp.float32


def index_of(y, z, c):
    return ((y % Y) * Z + z % Z) * C + c


def pairs(move, cores=(0, 1)):
    return [
        (index_of(y, z, c), index_of(*move(y, z, c)))
        for y in range(Y)
        for z in range(Z)
        for c in cores
    ]


def send(value, move, cores=(0, 1)):
    return lax.ppermute(value, "latent", pairs(move, cores))


def swap(value):
    return send(value, lambda y, z, c: (y, z, 1 - c))


def send_layer(value, steps):
    count = lax.axis_size("layer")
    sources = [s for s in range(count) if 0 <= s + steps < count]
    return lax.ppermute(value, "layer", [(s, s + steps) for s in sources])


def chip_rows(value, core):
    other = swap(value)
    return jnp.where(core == 0, jnp.concatenate([value, other]), jnp.concatenate([other, value]))


def spread(chip, core):
    near = [
        send(chip, lambda y, z, c, k=k: (y, z + k if c == 0 else z - k, c)) for k in (1, 2, 3)
    ]
    far = send(chip, lambda y, z, c: (y, z + 4, c), (1,))
    first = jnp.where(core == 0, chip, far)
    row = jnp.concatenate([first] + near)
    parts = [row] + [send(row, lambda y, z, c, k=k: (y + k, z, c)) for k in (1, 2, 3)]
    return jnp.concatenate(parts + [swap(part) for part in parts])


def collect(partial, core):
    width = partial.shape[-1]
    halves = partial.reshape(2, Y, 4 * 2 * 8, width)
    own = [
        (halves[0, k].astype(F32) + swap(halves[1, k]).astype(F32)).astype(BF) for k in range(Y)
    ]
    row = own[0].astype(F32)
    for k in (1, 2, 3):
        row = row + send(own[k], lambda y, z, c, k=k: (y - k, z, c)).astype(F32)
    row = row.astype(BF).reshape(4, 16, width)
    total = jnp.where(core == 0, row[0], send(row[0], lambda y, z, c: (y, z + 4, c), (1,)))
    total = total.astype(F32)
    for k in (1, 2, 3):
        piece = send(row[k], lambda y, z, c, k=k: (y, z - k if c == 0 else z + k, c))
        total = total + piece.astype(F32)
    total = total.astype(BF)
    return total.astype(F32) + swap(total).astype(F32)


def shard_chips(latent):
    y, z, c = latent // (Z * C), latent // C % Z, latent % C
    p = jnp.arange(Y * Z, dtype=jnp.int32)
    half, step, j = p // 16, p // 4 % 4, p % 4
    side = (half + c) % 2
    from_z = jnp.where(side == 0, z - j, jnp.where(j == 0, z + 4, z + j)) % Z
    return (y - step) % Y * Z + from_z


def shards(residual, target, enc_weight, enc_bias, dec_weight, active):
    layers = dec_weight.shape[0]
    width = residual.shape[-1]
    layer = lax.axis_index("layer")
    latent = lax.axis_index("latent")
    core = latent % C
    chips = shard_chips(latent)
    names = lax.dynamic_index_in_dim(active, layer, 0, keepdims=False)
    hit = jnp.any(names == latent, axis=1)
    tile = chips // 4
    live = jnp.any((tile[:, None] == jnp.arange(NTILE)[None, :]) & hit[None, :], axis=1)
    live = jnp.repeat(live, 16)[:, None]

    rows = spread(chip_rows(residual[0], core), core)
    goal = chip_rows(target[0], core)
    preact = jnp.dot(rows, enc_weight[0], preferred_element_type=F32) + enc_bias[0][None, :]
    on = live & (preact > 0)
    codes = jnp.where(on, preact, 0.0).astype(BF)
    dec = dec_weight[:, 0]
    sources = [codes] + [send_layer(codes, k) for k in range(1, layers)]
    weights = [
        lax.dynamic_index_in_dim(dec, (layer - k) % layers, 0, keepdims=False)
        for k in range(layers)
    ]
    partial = jnp.dot(
        jnp.concatenate(sources, axis=1), jnp.concatenate(weights), preferred_element_type=F32
    ).astype(BF)
    errors = collect(partial, core) - goal.astype(F32)
    full = spread(errors.astype(BF), core)

    backs = [
        lax.dot_general(full, weight, (((1,), (1,)), ((), ())), preferred_element_type=F32)
        for weight in weights
    ]
    mine = backs[0]
    for k in range(1, layers):
        mine = mine + send_layer(backs[k].astype(BF), -k).astype(F32)

    square = full.astype(F32).reshape(Y * Z, 16, width)
    square = jnp.sum(square * square, axis=(1, 2))
    place = chips[None, :] == jnp.arange(Y * Z)[:, None]
    square = jnp.sum(jnp.sum(jnp.where(place, square[None, :], 0.0), axis=1))
    square = jnp.full((8, 128), square)
    ring = [(s, (s + 1) % layers) for s in range(layers)]
    loss = jnp.zeros((layers, 8, 128), F32)
    moving = square
    for k in range(layers):
        loss = lax.dynamic_update_index_in_dim(loss, moving, (layer - k) % layers, 0)
        if k < layers - 1:
            moving = lax.ppermute(moving, "layer", ring)
    loss = loss[:, 0, 0]
    total = loss[0]
    for s in range(1, layers):
        total = total + loss[s]
    total = 0.5 * total / (layers * NTILE * TILE * width)

    placed = jnp.stack(
        [
            sum(
                jnp.where((layer - k) % layers == s, sources[k], jnp.zeros_like(codes))
                for k in range(layers)
            )
            for s in range(layers)
        ]
    )
    dec_grad = jnp.stack(
        [
            lax.dot_general(
                placed[s], full, (((0,), (0,)), ((), ())), preferred_element_type=F32
            )
            for s in range(layers)
        ]
    )
    dec_grad = (dec_grad / TILE).astype(BF)[:, None]
    pre_grad = jnp.where(on, mine, 0.0)
    bias_grad = (jnp.sum(pre_grad, axis=0) / TILE)[None]
    enc_grad = lax.dot_general(
        rows, pre_grad.astype(BF), (((0,), (0,)), ((), ())), preferred_element_type=F32
    )
    enc_grad = (enc_grad / TILE).astype(BF)[None]
    return (total, enc_grad, bias_grad, dec_grad)


def solution(mesh):
    in_specs = (
        P("layer", "latent", None),
        P("layer", "latent", None),
        P("layer", None, "latent"),
        P("layer", "latent"),
        P(None, "layer", "latent", None),
        P(),
    )
    out_specs = (
        P(),
        P("layer", None, "latent"),
        P("layer", "latent"),
        P(None, "layer", "latent", None),
    )
    return jax.shard_map(shards, mesh=mesh, in_specs=in_specs, out_specs=out_specs, check_vma=False)
```

```python
import jax
import jax.numpy as jnp
from jax import lax
from jax.sharding import PartitionSpec as P

TILE = 64
NTILE = 8
Y, Z, C = 4, 8, 2
BF = jnp.bfloat16
F32 = jnp.float32


def index_of(y, z, c):
    return ((y % Y) * Z + z % Z) * C + c


def pairs(move, cores=(0, 1)):
    return [
        (index_of(y, z, c), index_of(*move(y, z, c)))
        for y in range(Y)
        for z in range(Z)
        for c in cores
    ]


def send(value, move, cores=(0, 1)):
    return lax.ppermute(value, "latent", pairs(move, cores))


def swap(value):
    return send(value, lambda y, z, c: (y, z, 1 - c))


def send_layer(value, steps):
    count = lax.axis_size("layer")
    sources = [s for s in range(count) if 0 <= s + steps < count]
    return lax.ppermute(value, "layer", [(s, s + steps) for s in sources])


def chip_rows(value, core):
    other = swap(value)
    return jnp.where(core == 0, jnp.concatenate([value, other]), jnp.concatenate([other, value]))


def spread(chip, core):
    near = [
        send(chip, lambda y, z, c, k=k: (y, z + k if c == 0 else z - k, c)) for k in (1, 2, 3)
    ]
    far = send(chip, lambda y, z, c: (y, z + 4, c), (1,))
    half = jnp.concatenate([jnp.where(core == 0, chip, far)] + near)
    across = send(half, lambda y, z, c: (y + 2, z, c))
    row = jnp.concatenate([half, swap(half)])
    beside = send(row, lambda y, z, c: (y + 1 if c == 0 else y - 1, z, c))
    beside = jnp.concatenate([beside, swap(beside)])
    across = jnp.concatenate([across, swap(across)])
    return [row, beside, across]


def collect(partial, core):
    row, beside, across = partial
    count, width = row.shape
    half = count // 2
    beside = (beside[:count].astype(F32) + swap(beside[count:]).astype(F32)).astype(BF)
    beside = send(beside, lambda y, z, c: (y - 1 if c == 0 else y + 1, z, c))
    across = (across[:half].astype(F32) + swap(across[half:]).astype(F32)).astype(BF)
    across = send(across, lambda y, z, c: (y + 2, z, c))
    row = row.astype(F32) + beside.astype(F32)
    row = row[:half] + swap(row[half:].astype(BF)).astype(F32) + across.astype(F32)
    row = row.astype(BF).reshape(4, half // 4, width)
    far = send(row[0], lambda y, z, c: (y, z + 4, c), (1,))
    total = jnp.where(core == 0, row[0], far).astype(F32)
    for k in (1, 2, 3):
        piece = send(row[k], lambda y, z, c, k=k: (y, z - k if c == 0 else z + k, c))
        total = total + piece.astype(F32)
    total = total.astype(BF)
    return total.astype(F32) + swap(total).astype(F32)


def shard_chips(latent):
    y, z, c = latent // (Z * C), latent // C % Z, latent % C
    p = jnp.arange(Y * Z, dtype=jnp.int32)
    chunk, half, j = p // 8, p // 4 % 2, p % 4
    side = (half + c + (chunk == 2)) % 2
    step = 1 - 2 * c
    from_y = y + jnp.where(chunk == 1, -step, jnp.where(chunk == 2, step, jnp.where(chunk == 3, 2, 0)))
    from_z = jnp.where(side == 0, z - j, jnp.where(j == 0, z + 4, z + j)) % Z
    return from_y % Y * Z + from_z


def shards(residual, target, enc_weight, enc_bias, dec_weight, active):
    layers = dec_weight.shape[0]
    width = residual.shape[-1]
    layer = lax.axis_index("layer")
    latent = lax.axis_index("latent")
    core = latent % C
    chips = shard_chips(latent)
    names = lax.dynamic_index_in_dim(active, layer, 0, keepdims=False)
    hit = jnp.any(names == latent, axis=1)
    live = jnp.any((chips[:, None] // 4 == jnp.arange(NTILE)[None, :]) & hit[None, :], axis=1)
    live = jnp.repeat(live, 16)[:, None]
    dec = dec_weight[:, 0]
    weights = [
        lax.dynamic_index_in_dim(dec, (layer - k) % layers, 0, keepdims=False)
        for k in range(layers)
    ]

    inputs = spread(chip_rows(residual[0], core), core)
    goal = chip_rows(target[0], core)
    codes, on, partial = [], [], []
    start = 0
    for rows in inputs:
        preact = jnp.dot(rows, enc_weight[0], preferred_element_type=F32) + enc_bias[0][None, :]
        on.append(live[start : start + rows.shape[0]] & (preact > 0))
        start += rows.shape[0]
        own = jnp.where(on[-1], preact, 0.0).astype(BF)
        codes.append([own] + [send_layer(own, k) for k in range(1, layers)])
        partial.append(
            jnp.dot(
                jnp.concatenate(codes[-1], axis=1),
                jnp.concatenate(weights),
                preferred_element_type=F32,
            ).astype(BF)
        )
    errors = (collect(partial, core) - goal.astype(F32)).astype(BF)
    errors = spread(errors, core)

    mine = []
    for part in errors:
        backs = [
            lax.dot_general(part, weight, (((1,), (1,)), ((), ())), preferred_element_type=F32)
            for weight in weights
        ]
        total = backs[0]
        for k in range(1, layers):
            total = total + send_layer(backs[k].astype(BF), -k).astype(F32)
        mine.append(total)

    full = jnp.concatenate(errors)
    sources = [jnp.concatenate([part[k] for part in codes]) for k in range(layers)]
    placed = [
        sum(
            jnp.where((layer - k) % layers == s, sources[k], jnp.zeros_like(sources[k]))
            for k in range(layers)
        )
        for s in range(layers)
    ]
    dec_grad = lax.dot_general(
        jnp.concatenate(placed, axis=1),
        full,
        (((0,), (0,)), ((), ())),
        preferred_element_type=F32,
    )
    dec_grad = (dec_grad / TILE).astype(BF).reshape(layers, 1, -1, width)

    square = full.astype(F32).reshape(Y * Z, 16, width)
    square = jnp.sum(square * square, axis=(1, 2))
    place = chips[None, :] == jnp.arange(Y * Z)[:, None]
    square = jnp.sum(jnp.sum(jnp.where(place, square[None, :], 0.0), axis=1))
    square = jnp.full((8, 128), square)
    loss = jnp.zeros((layers, 8, 128), F32)
    for k in range(layers):
        ring = [(s, (s + k) % layers) for s in range(layers)]
        moved = lax.ppermute(square, "layer", ring) if k else square
        loss = lax.dynamic_update_index_in_dim(loss, moved, (layer - k) % layers, 0)
    total = loss[0]
    for s in range(1, layers):
        total = total + loss[s]
    total = 0.5 * total[0, 0] / (layers * NTILE * TILE * width)

    pre_grad = jnp.where(jnp.concatenate(on), jnp.concatenate(mine), 0.0)
    bias_grad = (jnp.sum(pre_grad, axis=0) / TILE)[None]
    enc_grad = lax.dot_general(
        jnp.concatenate(inputs),
        pre_grad.astype(BF),
        (((0,), (0,)), ((), ())),
        preferred_element_type=F32,
    )
    enc_grad = (enc_grad / TILE).astype(BF)[None]
    return (total, enc_grad, bias_grad, dec_grad)


def solution(mesh):
    in_specs = (
        P("layer", "latent", None),
        P("layer", "latent", None),
        P("layer", None, "latent"),
        P("layer", "latent"),
        P(None, "layer", "latent", None),
        P(),
    )
    out_specs = (
        P(),
        P("layer", None, "latent"),
        P("layer", "latent"),
        P(None, "layer", "latent", None),
    )
    return jax.shard_map(shards, mesh=mesh, in_specs=in_specs, out_specs=out_specs, check_vma=False)
```

```python
import functools

import jax
import jax.numpy as jnp
from jax import lax
from jax.experimental import pallas as pl
from jax.experimental.pallas import tpu as pltpu
from jax.sharding import PartitionSpec as P

TILE = 64
NTILE = 8
CAP = 6
Y, Z, C = 4, 8, 2
BF = jnp.bfloat16
F32 = jnp.float32
STEPS = (0, 1, 3, 2)


def index_of(y, z, c):
    return ((y % Y) * Z + z % Z) * C + c


def pairs(move, cores=(0, 1)):
    return [
        (index_of(y, z, c), index_of(*move(y, z, c)))
        for y in range(Y)
        for z in range(Z)
        for c in cores
    ]


def send(value, move, cores=(0, 1)):
    return lax.ppermute(value, "latent", pairs(move, cores))


def swap(value):
    return send(value, lambda y, z, c: (y, z, 1 - c))


def send_layer(value, steps):
    count = lax.axis_size("layer")
    sources = [s for s in range(count) if 0 <= s + steps < count]
    return lax.ppermute(value, "layer", [(s, s + steps) for s in sources])


def chip_rows(value, core):
    other = swap(value)
    return jnp.where(core == 0, jnp.concatenate([value, other]), jnp.concatenate([other, value]))


def spread_z(chip, core):
    near = [
        send(chip, lambda y, z, c, k=k: (y, z + k if c == 0 else z - k, c)) for k in (1, 2, 3)
    ]
    far = send(chip, lambda y, z, c: (y, z + 4, c), (1,))
    return jnp.concatenate([jnp.where(core == 0, chip, far)] + near)


def spread_y(half):
    parts = [half] + [send(half, lambda y, z, c, k=k: (y ^ k, z, c)) for k in STEPS[1:]]
    return parts, [swap(part) for part in parts]


def collect(halves, core):
    width = halves[0].shape[-1]
    halves = [half.reshape(Y, 4 * 2 * 8, width) for half in halves]
    own = [
        (halves[0][k].astype(F32) + swap(halves[1][k]).astype(F32)).astype(BF) for k in range(Y)
    ]
    row = own[0].astype(F32)
    for part, k in zip(own[1:], STEPS[1:]):
        row = row + send(part, lambda y, z, c, k=k: (y ^ k, z, c)).astype(F32)
    row = row.astype(BF).reshape(4, 16, width)
    far = send(row[0], lambda y, z, c: (y, z + 4, c), (1,))
    total = jnp.where(core == 0, row[0], far).astype(F32)
    for k in (1, 2, 3):
        piece = send(row[k], lambda y, z, c, k=k: (y, z - k if c == 0 else z + k, c))
        total = total + piece.astype(F32)
    total = total.astype(BF)
    return total.astype(F32) + swap(total).astype(F32)


def shard_chips(latent):
    y, z, c = latent // (Z * C), latent // C % Z, latent % C
    p = jnp.arange(Y * Z, dtype=jnp.int32)
    half, step, j = p // 16, p // 4 % 4, p % 4
    step = jnp.where(step < 2, step, 5 - step)
    side = (half + c) % 2
    from_z = jnp.where(side == 0, z - j, jnp.where(j == 0, z + 4, z + j)) % Z
    return (y ^ step) * Z + from_z


SMALL = pl.CostEstimate(flops=1000, bytes_accessed=1000, transcendentals=0)


def params(mib):
    return pltpu.CompilerParams(vmem_limit_bytes=mib * 1024 * 1024)


def join(parts, out_ref):
    at = 0
    for part in parts:
        out_ref[at : at + part.shape[0]] = part[...]
        at += part.shape[0]


def picked(slot, rows):
    at = lax.broadcasted_iota(jnp.int32, (CAP * TILE, rows), 0)
    return (at == slot).astype(F32).astype(BF)


def unpack(slot, packed):
    at = lax.broadcasted_iota(jnp.int32, (slot.shape[1], packed.shape[0]), 1)
    pick = (at == column(slot)).astype(F32).astype(BF)
    return jnp.dot(pick, packed, preferred_element_type=F32)


def column(row):
    return jnp.broadcast_to(row, (128, row.shape[1])).T[:, :1]


def early(halves):
    return [*halves[0][:-1], *halves[1][:-1]]


def late(halves):
    return [halves[0][-1], halves[1][-1]]


def early_late(row, rows_each):
    cut = 2 * rows_each - rows_each // 2
    return jnp.concatenate(
        [row[:, :cut], row[:, 2 * rows_each :][:, :cut], row[:, cut : 2 * rows_each]]
        + [row[:, 2 * rows_each + cut :]],
        axis=1,
    )


def encode_early_kernel(weight_ref, bias_ref, *refs):
    parts, (out_ref, rows_ref) = refs[:-2], refs[-2:]
    join(parts, rows_ref)
    out_ref[...] = (
        jnp.dot(rows_ref[...], weight_ref[...], preferred_element_type=F32) + bias_ref[...]
    )


def encode_early(weight, bias, parts):
    count = sum(part.shape[0] for part in parts)
    width, feats = weight.shape
    return pl.pallas_call(
        encode_early_kernel,
        out_shape=jax.ShapeDtypeStruct((count, feats), F32),
        scratch_shapes=[pltpu.VMEM((count, width), BF)],
        compiler_params=params(10),
        cost_estimate=SMALL,
        name="encode_early",
    )(weight, bias, *parts)


def encode_late_kernel(slot_ref, weight_ref, bias_ref, preact_ref, *refs):
    parts, (packed_ref, codes_ref, on_ref, rows_ref) = refs[:-4], refs[-4:]
    join(parts, rows_ref)
    last = jnp.dot(rows_ref[...], weight_ref[...], preferred_element_type=F32) + bias_ref[...]
    count = preact_ref.shape[0]
    slot = slot_ref[:1, :]
    live = column(slot) >= 0
    packed = None
    each, rest = count // 2, last.shape[0] // 2
    for preact, at, size in ((preact_ref[...], 0, each), (last, count, rest)):
        end = at + preact.shape[0]
        on = jnp.where(live[at:end] & (preact > 0), 1.0, 0.0)
        codes = jnp.where(on > 0, preact, 0.0).astype(BF)
        on = on.astype(BF)
        term = jnp.dot(picked(slot[:, at:end], end - at), codes, preferred_element_type=F32)
        packed = term if packed is None else packed + term
        for half in range(2):
            to = half * (each + rest) + (each if at else 0)
            codes_ref[to : to + size] = codes[half * size : half * size + size]
            on_ref[to : to + size] = on[half * size : half * size + size]
    packed_ref[...] = packed.astype(BF)


def encode_late(slot, weight, bias, preact, parts):
    count = sum(part.shape[0] for part in parts)
    width, feats = weight.shape
    total = preact.shape[0] + count
    return pl.pallas_call(
        encode_late_kernel,
        out_shape=[
            jax.ShapeDtypeStruct((CAP * TILE, feats), BF),
            jax.ShapeDtypeStruct((total, feats), BF),
            jax.ShapeDtypeStruct((total, feats), BF),
        ],
        scratch_shapes=[pltpu.VMEM((count, width), BF)],
        compiler_params=params(10),
        cost_estimate=SMALL,
        name="encode_late",
    )(slot, weight, bias, preact, *parts)


def turn_kernel(after_ref, *refs):
    parts, (out_ref, token_ref) = refs[:-2], refs[-2:]
    at = 0
    for first, second in zip(parts[0::2], parts[1::2]):
        both = jnp.concatenate([first[...], second[...]])
        out_ref[:, at : at + both.shape[0]] = both.T
        at += both.shape[0]
    token_ref[...] = after_ref[:16, :128]


def turn(parts, after):
    count = sum(part.shape[0] for part in parts)
    return pl.pallas_call(
        turn_kernel,
        out_shape=[
            jax.ShapeDtypeStruct((parts[0].shape[1], count), BF),
            jax.ShapeDtypeStruct((16, 128), BF),
        ],
        compiler_params=params(10),
        cost_estimate=SMALL,
        name="turn",
    )(after, *parts)


def dec_gradient_kernel(layer_ref, codes_ref, first_ref, second_ref, weight_ref, *refs):
    del layer_ref
    parts, (out_ref, own_ref, errors_ref) = refs[:-3], refs[-3:]
    over_rows = (((0,), (0,)), ((), ()))

    @pl.when(pl.program_id(0) == 0)
    def _():
        join(parts, errors_ref)
        own_ref[...] = lax.dot_general(
            errors_ref[...], weight_ref[...], (((1,), (1,)), ((), ())), preferred_element_type=F32
        )
        grad = lax.dot_general(
            codes_ref[...], errors_ref[...], over_rows, preferred_element_type=F32
        )
        out_ref[0] = (grad * (1.0 / TILE)).astype(BF)

    @pl.when(pl.program_id(0) > 0)
    def _():
        count = first_ref.shape[1]
        grad = lax.dot_general(
            first_ref[0], errors_ref[:count], over_rows, preferred_element_type=F32
        ) + lax.dot_general(
            second_ref[0], errors_ref[count:], over_rows, preferred_element_type=F32
        )
        out_ref[0] = (grad * (1.0 / TILE)).astype(BF)


def dec_gradient(layer, codes, first, second, weight, parts):
    layers = first.shape[0] + 1
    feats, width = weight.shape
    count = codes.shape[0]
    other = lambda k, at: (lax.max(k - 1, 0), 0, 0)
    whole = lambda array: pl.BlockSpec(array.shape, lambda k, at: (0,) * array.ndim)
    return pl.pallas_call(
        dec_gradient_kernel,
        grid_spec=pltpu.PrefetchScalarGridSpec(
            num_scalar_prefetch=1,
            grid=(layers,),
            in_specs=[
                whole(codes),
                pl.BlockSpec((1, *first.shape[1:]), other),
                pl.BlockSpec((1, *second.shape[1:]), other),
                whole(weight),
                *[whole(part) for part in parts],
            ],
            out_specs=[
                pl.BlockSpec(
                    (1, feats, width), lambda k, at: (lax.rem(at[0] - k + layers, layers), 0, 0)
                ),
                pl.BlockSpec((count, feats), lambda k, at: (0, 0)),
            ],
            scratch_shapes=[pltpu.VMEM((count, width), BF)],
        ),
        out_shape=[
            jax.ShapeDtypeStruct((layers, feats, width), BF),
            jax.ShapeDtypeStruct((count, feats), F32),
        ],
        compiler_params=params(20),
        cost_estimate=SMALL,
        name="dec_gradient",
    )(layer.reshape(1), codes, first, second, weight, *parts)


def add_squares(parts, out_ref, start):
    for part in parts:
        count, width = part.shape
        for at in range(0, count, 16):
            value = part[at : at + 16, :].astype(F32)
            value = value * value
            value = value[:8] + value[8:]
            total = value[:, :128]
            for lane in range(128, width, 128):
                total = total + value[:, lane : lane + 128]
            out_ref[start] = total
            start += 1


def back_early_kernel(layers, *refs):
    weights, parts = refs[: layers - 1], refs[layers - 1 : -3]
    out_ref, squares_ref, errors_ref = refs[-3:]
    join(parts, errors_ref)
    add_squares(parts, squares_ref, 0)
    for k in range(layers - 1):
        back = lax.dot_general(
            errors_ref[...],
            weights[k][...],
            (((1,), (1,)), ((), ())),
            preferred_element_type=F32,
        )
        out_ref[k] = back.astype(BF)


def back_early(weights, parts):
    count = sum(part.shape[0] for part in parts)
    feats, width = weights[0].shape
    return pl.pallas_call(
        functools.partial(back_early_kernel, len(weights) + 1),
        out_shape=[
            jax.ShapeDtypeStruct((len(weights), count, feats), BF),
            jax.ShapeDtypeStruct((count // 16, 8, 128), F32),
        ],
        scratch_shapes=[pltpu.VMEM((count, width), BF)],
        compiler_params=params(12),
        cost_estimate=SMALL,
        name="back_early",
    )(*weights, *parts)


def back_late_kernel(layers, place_ref, slot_ref, squares_ref, backs_ref, *refs):
    weights, refs = refs[: layers - 1], refs[layers - 1 :]
    parts, away = refs[: -layers - 1], refs[-layers - 1 : -2]
    errors_ref, sums_ref = refs[-2:]
    join(parts, errors_ref)
    count = squares_ref.shape[0]
    sums_ref[:count] = squares_ref[...]
    add_squares(parts, sums_ref, count)
    total = jnp.zeros((8, 128), F32)
    for chip in range(Y * Z):
        total = total + sums_ref[place_ref[chip]]
    left = jnp.broadcast_to(jnp.sum(total), (16, weights[0].shape[0]))
    row = lax.broadcasted_iota(jnp.int32, left.shape, 0)
    split = jnp.zeros(left.shape, F32)
    for k in range(3):
        piece = left.astype(BF).astype(F32)
        split = jnp.where(row == k, piece, split)
        left = left - piece
    packed = CAP * TILE
    before = backs_ref.shape[1]
    for k in range(1, layers):
        back = lax.dot_general(
            errors_ref[...],
            weights[k - 1][...],
            (((1,), (1,)), ((), ())),
            preferred_element_type=F32,
        )
        slot = slot_ref[k : k + 1, :]
        pick = picked(slot, slot.shape[1])
        here = jnp.dot(pick[:, :before], backs_ref[k - 1], preferred_element_type=F32)
        here = here + jnp.dot(pick[:, before:], back.astype(BF), preferred_element_type=F32)
        away[k - 1][:packed] = here.astype(BF)
        away[k - 1][packed:] = split.astype(BF)


def back_late(place, slot, squares, backs, weights, parts):
    layers = len(weights) + 1
    feats, width = weights[0].shape
    count = sum(part.shape[0] for part in parts)
    vmem = pl.BlockSpec(memory_space=pltpu.VMEM)
    return pl.pallas_call(
        functools.partial(back_late_kernel, layers),
        in_specs=[pl.BlockSpec(memory_space=pltpu.SMEM)]
        + [vmem] * (3 + len(weights) + len(parts)),
        out_specs=[vmem] * (layers - 1),
        out_shape=[jax.ShapeDtypeStruct((CAP * TILE + 16, feats), BF)] * (layers - 1),
        scratch_shapes=[pltpu.VMEM((count, width), BF), pltpu.VMEM((Y * Z, 8, 128), F32)],
        compiler_params=params(12),
        cost_estimate=SMALL,
        name="back_late",
    )(place, slot, squares, backs, *weights, *parts)


def decode_kernel(slot_ref, token_ref, codes_ref, *refs):
    del token_ref
    layers = (len(refs) - 1) // 2
    came, weights, out_ref, sources_ref = (
        refs[: layers - 1],
        refs[layers - 1 : 2 * layers - 1],
        refs[-2],
        refs[-1],
    )
    total = jnp.dot(codes_ref[...], weights[0][...], preferred_element_type=F32)
    for k in range(1, layers):
        source = unpack(slot_ref[k : k + 1, :], came[k - 1][...]).astype(BF)
        sources_ref[k - 1] = source
        total = total + jnp.dot(source, weights[k][...], preferred_element_type=F32)
    out_ref[...] = total.astype(BF)


def decode(slot, token, codes, came, weights):
    count, feats = codes.shape
    width = weights[0].shape[1]
    return pl.pallas_call(
        decode_kernel,
        out_shape=[
            jax.ShapeDtypeStruct((count, width), BF),
            jax.ShapeDtypeStruct((len(came), count, feats), BF),
        ],
        compiler_params=params(14),
        cost_estimate=SMALL,
        name="decode",
    )(slot, token, codes, *came, *weights)


def code_gradient_kernel(slot_ref, errors_ref, weight_ref, square_ref, out_ref):
    back = lax.dot_general(
        errors_ref[...], weight_ref[...], (((1,), (1,)), ((), ())), preferred_element_type=F32
    )
    count = CAP * TILE
    at = lax.broadcasted_iota(jnp.int32, (count, back.shape[0]), 0)
    pick = (at == slot_ref[...]).astype(F32).astype(BF)
    out_ref[:count] = jnp.dot(pick, back.astype(BF), preferred_element_type=F32).astype(BF)
    out_ref[count:] = square_ref[...]


def code_gradient(slot, errors, weight, square):
    return pl.pallas_call(
        code_gradient_kernel,
        out_shape=jax.ShapeDtypeStruct((CAP * TILE + 16, weight.shape[0]), BF),
        compiler_params=params(10),
        cost_estimate=SMALL,
        name="code_gradient",
    )(slot[None], errors, weight, square)


def enc_gradient_kernel(count, layer_ref, slot_ref, rows_ref, on_ref, own_ref, away_ref, *refs):
    came, (enc_ref, bias_ref, loss_ref, pre_ref) = refs[:-4], refs[-4:]
    packed = CAP * TILE
    layers = len(came) + 1

    @pl.when(pl.program_id(0) == 0)
    def _():
        total = own_ref[...]
        for k, ref in enumerate(came, 1):
            part = unpack(slot_ref[:1, :], ref[:packed])
            total = total + jnp.where(layer_ref[0] + k < layers, part, 0.0)
        total = jnp.where(on_ref[...] > 0, total, 0.0)
        bias_ref[...] = jnp.sum(total, axis=0, keepdims=True) * (1.0 / TILE)
        pre_ref[...] = total.astype(BF)
        sums = []
        for block in [ref[packed:] for ref in (away_ref, *came)]:
            block = block.astype(F32)
            sums.append(block[0:1] + block[1:2] + block[2:3])
        loss = jnp.zeros_like(sums[0])
        for s in range(layers):
            for k in range(layers):
                mine = lax.rem(layer_ref[0] + k, layers) == s
                loss = loss + jnp.where(mine, sums[k], 0.0)
        loss_ref[...] = loss[:, :1] * (0.5 / count)

    grad = jnp.dot(rows_ref[...], pre_ref[...], preferred_element_type=F32)
    enc_ref[...] = (grad * (1.0 / TILE)).astype(BF)


def enc_gradient(layer, slot, rows, on, own, away, came):
    width, count = rows.shape
    feats = own.shape[1]
    whole = lambda array: pl.BlockSpec(array.shape, lambda i: (0,) * array.ndim)
    part = width // 2
    return pl.pallas_call(
        functools.partial(enc_gradient_kernel, (len(came) + 1) * count * width),
        grid=(width // part,),
        in_specs=[
            pl.BlockSpec(memory_space=pltpu.SMEM),
            whole(slot),
            pl.BlockSpec((part, count), lambda i: (i, 0)),
            whole(on),
            whole(own),
            whole(away),
            *[whole(array) for array in came],
        ],
        out_specs=[
            pl.BlockSpec((part, feats), lambda i: (i, 0)),
            pl.BlockSpec((1, feats), lambda i: (0, 0)),
            pl.BlockSpec((1, 1), lambda i: (0, 0)),
        ],
        out_shape=[
            jax.ShapeDtypeStruct((width, feats), BF),
            jax.ShapeDtypeStruct((1, feats), F32),
            jax.ShapeDtypeStruct((1, 1), F32),
        ],
        scratch_shapes=[pltpu.VMEM((count, feats), BF)],
        compiler_params=params(12),
        cost_estimate=SMALL,
        name="enc_gradient",
    )(layer.reshape(1), slot, rows, on, own, away, *came)


def shards(residual, target, enc_weight, enc_bias, dec_weight, active):
    layers = dec_weight.shape[0]
    width = residual.shape[-1]
    layer = lax.axis_index("layer")
    latent = lax.axis_index("latent")
    core = latent % C

    half = spread_z(chip_rows(residual[0], core), core)
    half, target, dec, active = lax.optimization_barrier((half, target, dec_weight, active))
    rows = spread_y(half)

    chips = shard_chips(latent)
    hit = jnp.any(active == latent, axis=2)
    hit = jnp.stack(
        [
            lax.dynamic_index_in_dim(hit, (layer - k) % layers, 0, keepdims=False)
            for k in range(layers)
        ]
    )
    live = jnp.any(
        (chips[:, None] // 4 == jnp.arange(NTILE)[None, :])[None] & hit[:, None, :], axis=2
    )
    before = jnp.arange(Y * Z)[None, :] <= jnp.arange(Y * Z)[:, None]
    slot = jnp.sum(jnp.where(before[None] & live[:, None, :], 1, 0), axis=2) - 1
    slot = jnp.where(live, slot * 16, -TILE * NTILE)
    slot = jnp.repeat(slot, 16, axis=1) + jnp.tile(jnp.arange(16), Y * Z)[None, :]
    ordered = early_late(slot, TILE * NTILE // 4)
    place = jnp.sum(
        jnp.where(
            early_late(jnp.repeat(chips, 16)[None], TILE * NTILE // 4)[:, ::16]
            == jnp.arange(Y * Z)[:, None],
            jnp.arange(Y * Z)[None, :],
            0,
        ),
        axis=1,
        dtype=jnp.int32,
    )
    weights = [
        lax.dynamic_index_in_dim(dec[:, 0], (layer - k) % layers, 0, keepdims=False)
        for k in range(layers)
    ]
    goal = chip_rows(target[0], core)

    preact = encode_early(enc_weight[0], enc_bias, early(rows))
    packed, codes, on = encode_late(ordered, enc_weight[0], enc_bias, preact, late(rows))
    came = [send_layer(packed, k) for k in range(1, layers)]
    turned, token = turn([*rows[0], *rows[1]], packed)
    count = codes.shape[0] // 2
    partial, sources = zip(
        *[
            decode(slot[:, at : at + count], token, codes[at : at + count], came, weights)
            for at in (0, count)
        ]
    )
    errors = (collect(partial, core) - goal.astype(F32)).astype(BF)
    errors = spread_y(spread_z(errors, core))
    backs, squares = back_early(weights[1:], early(errors))
    away = back_late(place, ordered, squares, backs, weights[1:], late(errors))
    came = []
    for k in range(1, layers):
        ring = [(s, (s - k) % layers) for s in range(layers)]
        came.append(lax.ppermute(away[k - 1], "layer", ring))
    dec_grad, own = dec_gradient(layer, codes, *sources, weights[0], [*errors[0], *errors[1]])
    enc_grad, bias_grad, loss = enc_gradient(layer, slot, turned, on, own, away[0], came)
    loss = loss[0, 0]
    return (loss, enc_grad[None], bias_grad, dec_grad[:, None])


def solution(mesh):
    in_specs = (
        P("layer", "latent", None),
        P("layer", "latent", None),
        P("layer", None, "latent"),
        P("layer", "latent"),
        P(None, "layer", "latent", None),
        P(),
    )
    out_specs = (
        P(),
        P("layer", None, "latent"),
        P("layer", "latent"),
        P(None, "layer", "latent", None),
    )
    return jax.shard_map(shards, mesh=mesh, in_specs=in_specs, out_specs=out_specs, check_vma=False)
```

```python
import functools

import jax
import jax.numpy as jnp
from jax import lax
from jax.experimental import pallas as pl
from jax.experimental.pallas import tpu as pltpu
from jax.sharding import PartitionSpec as P

TILE = 64
NTILE = 8
CAP = 6
Y, Z, C = 4, 8, 2
BF = jnp.bfloat16
F32 = jnp.float32
STEPS = (0, 1, 3, 2)


def index_of(y, z, c):
    return ((y % Y) * Z + z % Z) * C + c


def pairs(move, cores=(0, 1)):
    return [
        (index_of(y, z, c), index_of(*move(y, z, c)))
        for y in range(Y)
        for z in range(Z)
        for c in cores
    ]


def send(value, move, cores=(0, 1)):
    return lax.ppermute(value, "latent", pairs(move, cores))


def swap(value):
    return send(value, lambda y, z, c: (y, z, 1 - c))


def send_layer(value, steps):
    count = lax.axis_size("layer")
    sources = [s for s in range(count) if 0 <= s + steps < count]
    return lax.ppermute(value, "layer", [(s, s + steps) for s in sources])


def chip_rows(value, core):
    other = swap(value)
    return jnp.where(core == 0, jnp.concatenate([value, other]), jnp.concatenate([other, value]))


def spread_z(chip, core):
    near = [
        send(chip, lambda y, z, c, k=k: (y, z ^ (k + 4 * c), c)) for k in (1, 2, 3)
    ]
    far = send(chip, lambda y, z, c: (y, z ^ 4, c), (1,))
    return jnp.concatenate([jnp.where(core == 0, chip, far)] + near)


def spread_y(half):
    parts = [half] + [send(half, lambda y, z, c, k=k: (y ^ k, z, c)) for k in STEPS[1:]]
    return parts + [swap(part) for part in parts]


def collect(halves, core):
    width = halves[0].shape[-1]
    halves = [half.reshape(Y, 4 * 2 * 8, width) for half in halves]
    own = [
        (halves[0][k].astype(F32) + swap(halves[1][k]).astype(F32)).astype(BF) for k in range(Y)
    ]
    row = own[0].astype(F32)
    for part, k in zip(own[1:], STEPS[1:]):
        row = row + send(part, lambda y, z, c, k=k: (y ^ k, z, c)).astype(F32)
    row = row.astype(BF).reshape(4, 16, width)
    far = send(row[0], lambda y, z, c: (y, z ^ 4, c), (1,))
    total = jnp.where(core == 0, row[0], far).astype(F32)
    for k in (1, 2, 3):
        piece = send(row[k], lambda y, z, c, k=k: (y, z ^ (k + 4 * c), c))
        total = total + piece.astype(F32)
    total = total.astype(BF)
    return total.astype(F32) + swap(total).astype(F32)


def shard_chips(latent):
    y, z, c = latent // (Z * C), latent // C % Z, latent % C
    p = jnp.arange(Y * Z, dtype=jnp.int32)
    half, step, j = p // 16, p // 4 % 4, p % 4
    step = jnp.where(step < 2, step, 5 - step)
    side = (half + c) % 2
    from_z = z ^ (j + 4 * side)
    return (y ^ step) * Z + from_z


SMALL = pl.CostEstimate(flops=1000, bytes_accessed=1000, transcendentals=0)


def params(mib):
    return pltpu.CompilerParams(vmem_limit_bytes=mib * 1024 * 1024)


def join(parts, out_ref):
    at = 0
    for part in parts:
        out_ref[at : at + part.shape[0]] = part[...]
        at += part.shape[0]


def pack(source_ref, k, value_ref, out_ref):
    for place in range(CAP * TILE // 16):
        start = pl.multiple_of(source_ref[k, place] * 16, 16)
        out_ref[place * 16 : place * 16 + 16, :] = value_ref[pl.ds(start, 16), :]


def unpacked(slot_ref, k, shard, packed_ref):
    slot = slot_ref[k, shard]
    start = pl.multiple_of(lax.max(slot, 0) * 16, 16)
    value = packed_ref[pl.ds(start, 16), :]
    return jnp.where(slot >= 0, value, jnp.zeros_like(value))


def encode_kernel(slot_ref, source_ref, weight_ref, bias_ref, *refs):
    parts, (packed_ref, codes_ref, on_ref, rows_ref) = refs[:-4], refs[-4:]
    join(parts, rows_ref)
    preact = jnp.dot(rows_ref[...], weight_ref[...], preferred_element_type=F32) + bias_ref[...]
    for shard in range(Y * Z):
        at = slice(shard * 16, shard * 16 + 16)
        on = jnp.where((preact[at] > 0) & (slot_ref[0, shard] >= 0), 1.0, 0.0)
        codes_ref[at, :] = jnp.where(on > 0, preact[at], 0.0).astype(BF)
        on_ref[at, :] = on.astype(BF)
    pack(source_ref, 0, codes_ref, packed_ref)


def specs(scalars, arrays):
    return [pl.BlockSpec(memory_space=pltpu.SMEM)] * scalars + [
        pl.BlockSpec(memory_space=pltpu.VMEM)
    ] * arrays


def encode(slot, source, weight, bias, parts):
    count = sum(part.shape[0] for part in parts)
    width, feats = weight.shape
    return pl.pallas_call(
        encode_kernel,
        in_specs=specs(2, 2 + len(parts)),
        out_shape=[
            jax.ShapeDtypeStruct((CAP * TILE, feats), BF),
            jax.ShapeDtypeStruct((count, feats), BF),
            jax.ShapeDtypeStruct((count, feats), BF),
        ],
        scratch_shapes=[pltpu.VMEM((count, width), BF)],
        compiler_params=params(10),
        cost_estimate=SMALL,
        name="encode",
    )(slot, source, weight, bias, *parts)


def turn_kernel(after_ref, *refs):
    parts, (out_ref, token_ref) = refs[:-2], refs[-2:]
    at = 0
    for first, second in zip(parts[0::2], parts[1::2]):
        both = jnp.concatenate([first[...], second[...]])
        out_ref[:, at : at + both.shape[0]] = both.T
        at += both.shape[0]
    token_ref[...] = after_ref[:16, :128]


def turn(parts, after):
    count = sum(part.shape[0] for part in parts)
    return pl.pallas_call(
        turn_kernel,
        out_shape=[
            jax.ShapeDtypeStruct((parts[0].shape[1], count), BF),
            jax.ShapeDtypeStruct((16, 128), BF),
        ],
        compiler_params=params(10),
        cost_estimate=SMALL,
        name="turn",
    )(after, *parts)


def dec_gradient_kernel(layer_ref, codes_ref, first_ref, second_ref, weight_ref, *refs):
    del layer_ref
    parts, (out_ref, own_ref, errors_ref) = refs[:-3], refs[-3:]
    over_rows = (((0,), (0,)), ((), ()))

    @pl.when(pl.program_id(0) == 0)
    def _():
        join(parts, errors_ref)
        own_ref[...] = lax.dot_general(
            errors_ref[...], weight_ref[...], (((1,), (1,)), ((), ())), preferred_element_type=F32
        )
        grad = lax.dot_general(
            codes_ref[...], errors_ref[...], over_rows, preferred_element_type=F32
        )
        out_ref[0] = (grad * (1.0 / TILE)).astype(BF)

    @pl.when(pl.program_id(0) > 0)
    def _():
        count = first_ref.shape[1]
        grad = lax.dot_general(
            first_ref[0], errors_ref[:count], over_rows, preferred_element_type=F32
        ) + lax.dot_general(
            second_ref[0], errors_ref[count:], over_rows, preferred_element_type=F32
        )
        out_ref[0] = (grad * (1.0 / TILE)).astype(BF)


def dec_gradient(layer, codes, first, second, weight, parts):
    layers = first.shape[0] + 1
    feats, width = weight.shape
    count = codes.shape[0]
    other = lambda k, at: (lax.max(k - 1, 0), 0, 0)
    whole = lambda array: pl.BlockSpec(array.shape, lambda k, at: (0,) * array.ndim)
    return pl.pallas_call(
        dec_gradient_kernel,
        grid_spec=pltpu.PrefetchScalarGridSpec(
            num_scalar_prefetch=1,
            grid=(layers,),
            in_specs=[
                whole(codes),
                pl.BlockSpec((1, *first.shape[1:]), other),
                pl.BlockSpec((1, *second.shape[1:]), other),
                whole(weight),
                *[whole(part) for part in parts],
            ],
            out_specs=[
                pl.BlockSpec(
                    (1, feats, width), lambda k, at: (lax.rem(at[0] - k + layers, layers), 0, 0)
                ),
                pl.BlockSpec((count, feats), lambda k, at: (0, 0)),
            ],
            scratch_shapes=[pltpu.VMEM((count, width), BF)],
        ),
        out_shape=[
            jax.ShapeDtypeStruct((layers, feats, width), BF),
            jax.ShapeDtypeStruct((count, feats), F32),
        ],
        compiler_params=params(20),
        cost_estimate=SMALL,
        name="dec_gradient",
    )(layer.reshape(1), codes, first, second, weight, *parts)


def add_squares(parts, out_ref, start):
    for part in parts:
        count, width = part.shape
        for at in range(0, count, 16):
            value = part[at : at + 16, :].astype(F32)
            value = value * value
            value = value[:8] + value[8:]
            total = value[:, :128]
            for lane in range(128, width, 128):
                total = total + value[:, lane : lane + 128]
            out_ref[start] = total
            start += 1


def back_kernel(layers, place_ref, source_ref, *refs):
    weights, refs = refs[: layers - 1], refs[layers - 1 :]
    away, errors_ref, back_ref, sums_ref = refs[-layers - 2 : -3], refs[-3], refs[-2], refs[-1]
    parts = refs[: -layers - 2]
    join(parts, errors_ref)
    packed = CAP * TILE
    for k in range(1, layers):
        back_ref[k - 1] = lax.dot_general(
            errors_ref[...],
            weights[k - 1][...],
            (((1,), (1,)), ((), ())),
            preferred_element_type=F32,
        ).astype(BF)
        pack(source_ref, k, back_ref.at[k - 1], away[k - 1])
    add_squares(parts, sums_ref, 0)
    total = jnp.zeros((8, 128), F32)
    for chip in range(Y * Z):
        total = total + sums_ref[place_ref[chip]]
    left = jnp.broadcast_to(jnp.sum(total), (16, weights[0].shape[0]))
    row = lax.broadcasted_iota(jnp.int32, left.shape, 0)
    split = jnp.zeros(left.shape, F32)
    for k in range(3):
        piece = left.astype(BF).astype(F32)
        split = jnp.where(row == k, piece, split)
        left = left - piece
    for ref in away:
        ref[packed:, :] = split.astype(BF)


def back(place, source, weights, parts):
    layers = len(weights) + 1
    feats, width = weights[0].shape
    count = sum(part.shape[0] for part in parts)
    return pl.pallas_call(
        functools.partial(back_kernel, layers),
        in_specs=specs(2, len(weights) + len(parts)),
        out_shape=[jax.ShapeDtypeStruct((CAP * TILE + 16, feats), BF)] * (layers - 1),
        scratch_shapes=[
            pltpu.VMEM((count, width), BF),
            pltpu.VMEM((layers - 1, count, feats), BF),
            pltpu.VMEM((Y * Z, 8, 128), F32),
        ],
        compiler_params=params(14),
        cost_estimate=SMALL,
        name="back",
    )(place, source, *weights, *parts)


def decode_kernel(half, slot_ref, token_ref, codes_ref, *refs):
    del token_ref
    layers = (len(refs) - 1) // 2
    came, weights = refs[: layers - 1], refs[layers - 1 : 2 * layers - 1]
    out_ref, sources_ref = refs[-2:]
    count = out_ref.shape[0]
    total = jnp.dot(
        codes_ref[half * count : half * count + count, :],
        weights[0][...],
        preferred_element_type=F32,
    )
    shards_of = count // 16
    for k in range(1, layers):
        for shard in range(shards_of):
            sources_ref[k - 1, shard * 16 : shard * 16 + 16, :] = unpacked(
                slot_ref, k, half * shards_of + shard, came[k - 1]
            )
        total = total + jnp.dot(
            sources_ref[k - 1], weights[k][...], preferred_element_type=F32
        )
    out_ref[...] = total.astype(BF)


def decode(half, slot, token, codes, came, weights):
    count, feats = codes.shape[0] // 2, codes.shape[1]
    width = weights[0].shape[1]
    return pl.pallas_call(
        functools.partial(decode_kernel, half),
        in_specs=specs(1, 2 + len(came) + len(weights)),
        out_shape=[
            jax.ShapeDtypeStruct((count, width), BF),
            jax.ShapeDtypeStruct((len(came), count, feats), BF),
        ],
        compiler_params=params(14),
        cost_estimate=SMALL,
        name="decode",
    )(slot, token, codes, *came, *weights)


def enc_gradient_kernel(count, layer_ref, slot_ref, rows_ref, on_ref, own_ref, away_ref, *refs):
    came, (enc_ref, bias_ref, loss_ref, pre_ref) = refs[:-4], refs[-4:]
    packed = CAP * TILE
    layers = len(came) + 1

    @pl.when(pl.program_id(0) == 0)
    def _():
        pieces = []
        for shard in range(own_ref.shape[0] // 16):
            piece = own_ref[shard * 16 : shard * 16 + 16, :]
            for k, ref in enumerate(came, 1):
                part = unpacked(slot_ref, 0, shard, ref).astype(F32)
                piece = piece + jnp.where(layer_ref[0] + k < layers, part, 0.0)
            pieces.append(piece)
        total = jnp.concatenate(pieces)
        total = jnp.where(on_ref[...] > 0, total, 0.0)
        bias_ref[...] = jnp.sum(total, axis=0, keepdims=True) * (1.0 / TILE)
        pre_ref[...] = total.astype(BF)
        sums = []
        for block in [ref[packed:] for ref in (away_ref, *came)]:
            block = block.astype(F32)
            sums.append(block[0:1] + block[1:2] + block[2:3])
        loss = jnp.zeros_like(sums[0])
        for s in range(layers):
            for k in range(layers):
                mine = lax.rem(layer_ref[0] + k, layers) == s
                loss = loss + jnp.where(mine, sums[k], 0.0)
        loss_ref[...] = loss[:, :1] * (0.5 / count)

    grad = jnp.dot(rows_ref[...], pre_ref[...], preferred_element_type=F32)
    enc_ref[...] = (grad * (1.0 / TILE)).astype(BF)


def enc_gradient(layer, slot, rows, on, own, away, came):
    width, count = rows.shape
    feats = own.shape[1]
    whole = lambda array: pl.BlockSpec(array.shape, lambda i: (0,) * array.ndim)
    part = width // 2
    return pl.pallas_call(
        functools.partial(enc_gradient_kernel, (len(came) + 1) * count * width),
        grid=(width // part,),
        in_specs=[
            pl.BlockSpec(memory_space=pltpu.SMEM),
            pl.BlockSpec(memory_space=pltpu.SMEM),
            pl.BlockSpec((part, count), lambda i: (i, 0)),
            whole(on),
            whole(own),
            whole(away),
            *[whole(array) for array in came],
        ],
        out_specs=[
            pl.BlockSpec((part, feats), lambda i: (i, 0)),
            pl.BlockSpec((1, feats), lambda i: (0, 0)),
            pl.BlockSpec((1, 1), lambda i: (0, 0)),
        ],
        out_shape=[
            jax.ShapeDtypeStruct((width, feats), BF),
            jax.ShapeDtypeStruct((1, feats), F32),
            jax.ShapeDtypeStruct((1, 1), F32),
        ],
        scratch_shapes=[pltpu.VMEM((count, feats), BF)],
        compiler_params=params(12),
        cost_estimate=SMALL,
        name="enc_gradient",
    )(layer.reshape(1), slot, rows, on, own, away, *came)


def shards(residual, target, enc_weight, enc_bias, dec_weight, active):
    layers = dec_weight.shape[0]
    width = residual.shape[-1]
    layer = lax.axis_index("layer")
    latent = lax.axis_index("latent")
    core = latent % C

    half = spread_z(chip_rows(residual[0], core), core)
    half, target, dec, active = lax.optimization_barrier((half, target, dec_weight, active))
    rows = spread_y(half)

    chips = shard_chips(latent)
    hit = jnp.any(active == latent, axis=2)
    hit = jnp.stack(
        [
            lax.dynamic_index_in_dim(hit, (layer - k) % layers, 0, keepdims=False)
            for k in range(layers)
        ]
    )
    live = jnp.any(
        (chips[:, None] // 4 == jnp.arange(NTILE)[None, :])[None] & hit[:, None, :], axis=2
    )
    every = jnp.arange(Y * Z)
    before = every[None, :] <= every[:, None]
    slot = jnp.sum(jnp.where(before[None] & live[:, None, :], 1, 0), axis=2, dtype=jnp.int32) - 1
    slot = jnp.where(live, jnp.minimum(slot, CAP * 4 - 1), -1)
    source = jnp.sum(
        jnp.where(slot[:, None, :] == jnp.arange(CAP * 4)[None, :, None], every, 0),
        axis=2,
        dtype=jnp.int32,
    )
    source = jnp.minimum(source, Y * Z - 1)
    place = jnp.sum(
        jnp.where(chips[None, :] == every[:, None], every[None, :], 0), axis=1, dtype=jnp.int32
    )
    weights = [
        lax.dynamic_index_in_dim(dec[:, 0], (layer - k) % layers, 0, keepdims=False)
        for k in range(layers)
    ]
    goal = chip_rows(target[0], core)

    packed, codes, on = encode(slot, source, enc_weight[0], enc_bias, rows)
    came = [send_layer(packed, k) for k in range(1, layers)]
    turned, token = turn(rows, packed)
    goal, token = lax.optimization_barrier((goal, token))
    partial, sources = zip(
        *[decode(half, slot, token, codes, came, weights) for half in range(2)]
    )
    errors = (collect(partial, core) - goal.astype(F32)).astype(BF)
    errors = spread_y(spread_z(errors, core))
    away = back(place, source, weights[1:], errors)
    came = []
    for k in range(1, layers):
        ring = [(s, (s - k) % layers) for s in range(layers)]
        came.append(lax.ppermute(away[k - 1], "layer", ring))
    dec_grad, own = dec_gradient(layer, codes, *sources, weights[0], errors)
    enc_grad, bias_grad, loss = enc_gradient(layer, slot, turned, on, own, away[0], came)
    loss = loss[0, 0]
    return (loss, enc_grad[None], bias_grad, dec_grad[:, None])


def solution(mesh):
    in_specs = (
        P("layer", "latent", None),
        P("layer", "latent", None),
        P("layer", None, "latent"),
        P("layer", "latent"),
        P(None, "layer", "latent", None),
        P(),
    )
    out_specs = (
        P(),
        P("layer", None, "latent"),
        P("layer", "latent"),
        P(None, "layer", "latent", None),
    )
    return jax.shard_map(shards, mesh=mesh, in_specs=in_specs, out_specs=out_specs, check_vma=False)
```

```python
import functools

import jax
import jax.numpy as jnp
from jax import lax
from jax.experimental import pallas as pl
from jax.experimental.pallas import tpu as pltpu
from jax.sharding import PartitionSpec as P

TILE = 64
NTILE = 8
CAP = 6
Y, Z, C = 4, 8, 2
BF = jnp.bfloat16
F32 = jnp.float32
STEPS = (0, 2, 1, 3)
ORDER = (2, 1, 3)


def index_of(y, z, c):
    return ((y % Y) * Z + z % Z) * C + c


def pairs(move, cores=(0, 1)):
    return [
        (index_of(y, z, c), index_of(*move(y, z, c)))
        for y in range(Y)
        for z in range(Z)
        for c in cores
    ]


def send(value, move, cores=(0, 1)):
    return lax.ppermute(value, "latent", pairs(move, cores))


def swap(value):
    return send(value, lambda y, z, c: (y, z, 1 - c))


def send_layer(value, steps):
    count = lax.axis_size("layer")
    sources = [s for s in range(count) if 0 <= s + steps < count]
    return lax.ppermute(value, "layer", [(s, s + steps) for s in sources])


def chip_rows(value, core):
    other = swap(value)
    return jnp.where(core == 0, jnp.concatenate([value, other]), jnp.concatenate([other, value]))


def spread_z(chip, core):
    near = [
        send(chip, lambda y, z, c, k=k: (y, z ^ (k + 4 * c), c)) for k in (1, 2, 3)
    ]
    far = send(chip, lambda y, z, c: (y, z ^ 4, c), (1,))
    return jnp.concatenate([jnp.where(core == 0, chip, far)] + near)


def spread_y(half):
    parts = [half] + [send(half, lambda y, z, c, k=k: (y ^ k, z, c)) for k in STEPS[1:]]
    return parts + [swap(part) for part in parts]


def collect(halves, core):
    width = halves[0].shape[-1]
    halves = [half.reshape(Y, 4 * 2 * 8, width) for half in halves]
    own = [
        (halves[0][k].astype(F32) + swap(halves[1][k]).astype(F32)).astype(BF) for k in range(Y)
    ]
    row = own[0].astype(F32)
    for part, k in zip(own[1:], STEPS[1:]):
        row = row + send(part, lambda y, z, c, k=k: (y ^ k, z, c)).astype(F32)
    row = row.astype(BF).reshape(4, 16, width)
    far = send(row[0], lambda y, z, c: (y, z ^ 4, c), (1,))
    total = jnp.where(core == 0, row[0], far).astype(F32)
    for k in (1, 2, 3):
        piece = send(row[k], lambda y, z, c, k=k: (y, z ^ (k + 4 * c), c))
        total = total + piece.astype(F32)
    total = total.astype(BF)
    return total.astype(F32) + swap(total).astype(F32)


def shard_chips(latent):
    y, z, c = latent // (Z * C), latent // C % Z, latent % C
    p = jnp.arange(Y * Z, dtype=jnp.int32)
    half, step, j = p // 16, p // 4 % 4, p % 4
    step = sum(jnp.where(step == i, to, 0) for i, to in enumerate(STEPS))
    side = (half + c) % 2
    from_z = z ^ (j + 4 * side)
    return (y ^ step) * Z + from_z


SMALL = pl.CostEstimate(flops=1000, bytes_accessed=1000, transcendentals=0)


def params(mib):
    return pltpu.CompilerParams(vmem_limit_bytes=mib * 1024 * 1024)


def join(parts, out_ref):
    at = 0
    for part in parts:
        out_ref[at : at + part.shape[0]] = part[...]
        at += part.shape[0]


def pack(source_ref, k, value_ref, out_ref):
    for place in range(CAP * TILE // 16):
        start = pl.multiple_of(source_ref[k, place] * 16, 16)
        out_ref[place * 16 : place * 16 + 16, :] = value_ref[pl.ds(start, 16), :]


def unpacked(slot_ref, k, shard, packed_ref):
    slot = slot_ref[k, shard]
    start = pl.multiple_of(lax.max(slot, 0) * 16, 16)
    value = packed_ref[pl.ds(start, 16), :]
    return jnp.where(slot >= 0, value, jnp.zeros_like(value))


def encode_kernel(slot_ref, source_ref, weight_ref, bias_ref, *refs):
    parts, (packed_ref, codes_ref, on_ref, rows_ref) = refs[:-4], refs[-4:]
    join(parts, rows_ref)
    preact = jnp.dot(rows_ref[...], weight_ref[...], preferred_element_type=F32) + bias_ref[...]
    for shard in range(Y * Z):
        at = slice(shard * 16, shard * 16 + 16)
        on = jnp.where((preact[at] > 0) & (slot_ref[0, shard] >= 0), 1.0, 0.0)
        codes_ref[at, :] = jnp.where(on > 0, preact[at], 0.0).astype(BF)
        on_ref[at, :] = on.astype(BF)
    pack(source_ref, 0, codes_ref, packed_ref)


def specs(scalars, arrays):
    return [pl.BlockSpec(memory_space=pltpu.SMEM)] * scalars + [
        pl.BlockSpec(memory_space=pltpu.VMEM)
    ] * arrays


def encode(slot, source, weight, bias, parts):
    count = sum(part.shape[0] for part in parts)
    width, feats = weight.shape
    return pl.pallas_call(
        encode_kernel,
        in_specs=specs(2, 2 + len(parts)),
        out_shape=[
            jax.ShapeDtypeStruct((CAP * TILE, feats), BF),
            jax.ShapeDtypeStruct((count, feats), BF),
            jax.ShapeDtypeStruct((count, feats), BF),
        ],
        scratch_shapes=[pltpu.VMEM((count, width), BF)],
        compiler_params=params(10),
        cost_estimate=SMALL,
        name="encode",
    )(slot, source, weight, bias, *parts)


def turn_kernel(after_ref, *refs):
    parts, (out_ref, token_ref) = refs[:-2], refs[-2:]
    at = 0
    for first, second in zip(parts[0::2], parts[1::2]):
        both = jnp.concatenate([first[...], second[...]])
        out_ref[:, at : at + both.shape[0]] = both.T
        at += both.shape[0]
    token_ref[...] = after_ref[:16, :128]


def turn(parts, after):
    count = sum(part.shape[0] for part in parts)
    return pl.pallas_call(
        turn_kernel,
        out_shape=[
            jax.ShapeDtypeStruct((parts[0].shape[1], count), BF),
            jax.ShapeDtypeStruct((16, 128), BF),
        ],
        compiler_params=params(10),
        cost_estimate=SMALL,
        name="turn",
    )(after, *parts)


def dec_gradient_kernel(layer_ref, first_ref, second_ref, weight_ref, *refs):
    del layer_ref
    parts, (out_ref, own_ref, errors_ref) = refs[:-3], refs[-3:]

    @pl.when(pl.program_id(0) == 0)
    def _():
        join(parts, errors_ref)
        own_ref[...] = lax.dot_general(
            errors_ref[...], weight_ref[...], (((1,), (1,)), ((), ())), preferred_element_type=F32
        )

    codes = jnp.concatenate([first_ref[...], second_ref[...]])
    grad = lax.dot_general(
        codes, errors_ref[...], (((0,), (0,)), ((), ())), preferred_element_type=F32
    )
    out_ref[0] = (grad * (1.0 / TILE)).astype(BF)


def dec_gradient(layer, layers, first, second, weight, parts):
    depth, width = weight.shape
    feats = depth // layers
    count = first.shape[0] + second.shape[0]
    whole = lambda array: pl.BlockSpec(array.shape, lambda k, at: (0,) * array.ndim)
    return pl.pallas_call(
        dec_gradient_kernel,
        grid_spec=pltpu.PrefetchScalarGridSpec(
            num_scalar_prefetch=1,
            grid=(layers,),
            in_specs=[
                pl.BlockSpec((first.shape[0], feats), lambda k, at: (0, k)),
                pl.BlockSpec((second.shape[0], feats), lambda k, at: (0, k)),
                pl.BlockSpec((feats, width), lambda k, at: (0, 0)),
                *[whole(part) for part in parts],
            ],
            out_specs=[
                pl.BlockSpec(
                    (1, feats, width), lambda k, at: (lax.rem(at[0] - k + layers, layers), 0, 0)
                ),
                pl.BlockSpec((count, feats), lambda k, at: (0, 0)),
            ],
            scratch_shapes=[pltpu.VMEM((count, width), BF)],
        ),
        out_shape=[
            jax.ShapeDtypeStruct((layers, feats, width), BF),
            jax.ShapeDtypeStruct((count, feats), F32),
        ],
        compiler_params=params(20),
        cost_estimate=SMALL,
        name="dec_gradient",
    )(layer.reshape(1), first, second, weight, *parts)


def add_squares(parts, out_ref, start):
    for part in parts:
        count, width = part.shape
        for at in range(0, count, 16):
            value = part[at : at + 16, :].astype(F32)
            value = value * value
            value = value[:8] + value[8:]
            total = value[:, :128]
            for lane in range(128, width, 128):
                total = total + value[:, lane : lane + 128]
            out_ref[start] = total
            start += 1


def back_kernel(layers, place_ref, source_ref, weight_ref, *refs):
    feats = weight_ref.shape[0] // layers
    away, errors_ref, back_ref, sums_ref = refs[-layers - 2 : -3], refs[-3], refs[-2], refs[-1]
    parts = refs[: -layers - 2]
    join(parts, errors_ref)
    packed = CAP * TILE
    for at, k in enumerate(ORDER):
        back_ref[at] = lax.dot_general(
            errors_ref[...],
            weight_ref[k * feats : (k + 1) * feats, :],
            (((1,), (1,)), ((), ())),
            preferred_element_type=F32,
        ).astype(BF)
        pack(source_ref, k, back_ref.at[at], away[at])
    add_squares(parts, sums_ref, 0)
    total = jnp.zeros((8, 128), F32)
    for chip in range(Y * Z):
        total = total + sums_ref[place_ref[chip]]
    left = jnp.broadcast_to(jnp.sum(total), (16, feats))
    row = lax.broadcasted_iota(jnp.int32, left.shape, 0)
    split = jnp.zeros(left.shape, F32)
    for k in range(3):
        piece = left.astype(BF).astype(F32)
        split = jnp.where(row == k, piece, split)
        left = left - piece
    for ref in away:
        ref[packed:, :] = split.astype(BF)


def back(place, source, layers, weight, parts):
    feats, width = weight.shape[0] // layers, weight.shape[1]
    count = sum(part.shape[0] for part in parts)
    return pl.pallas_call(
        functools.partial(back_kernel, layers),
        in_specs=specs(2, 1 + len(parts)),
        out_shape=[jax.ShapeDtypeStruct((CAP * TILE + 16, feats), BF)] * (layers - 1),
        scratch_shapes=[
            pltpu.VMEM((count, width), BF),
            pltpu.VMEM((layers - 1, count, feats), BF),
            pltpu.VMEM((Y * Z, 8, 128), F32),
        ],
        compiler_params=params(14),
        cost_estimate=SMALL,
        name="back",
    )(place, source, weight, *parts)


def decode_kernel(half, slot_ref, token_ref, codes_ref, weight_ref, *refs):
    del token_ref
    came, (out_ref, sources_ref) = refs[:-2], refs[-2:]
    count, feats = out_ref.shape[0], codes_ref.shape[1]
    sources_ref[:, :feats] = codes_ref[half * count : half * count + count, :]
    shards_of = count // 16
    for k, ref in zip(ORDER, came):
        for shard in range(shards_of):
            sources_ref[shard * 16 : shard * 16 + 16, k * feats : (k + 1) * feats] = unpacked(
                slot_ref, k, half * shards_of + shard, ref
            )
    out_ref[...] = jnp.dot(
        sources_ref[...], weight_ref[...], preferred_element_type=F32
    ).astype(BF)


def decode(half, slot, token, codes, came, weight):
    count = codes.shape[0] // 2
    depth, width = weight.shape
    return pl.pallas_call(
        functools.partial(decode_kernel, half),
        in_specs=specs(1, 3 + len(came)),
        out_shape=[
            jax.ShapeDtypeStruct((count, width), BF),
            jax.ShapeDtypeStruct((count, depth), BF),
        ],
        compiler_params=params(14),
        cost_estimate=SMALL,
        name="decode",
    )(slot, token, codes, weight, *came)


def enc_gradient_kernel(count, layer_ref, slot_ref, rows_ref, on_ref, own_ref, away_ref, *refs):
    came, (enc_ref, bias_ref, loss_ref, pre_ref) = refs[:-4], refs[-4:]
    packed = CAP * TILE
    layers = len(came) + 1

    @pl.when(pl.program_id(0) == 0)
    def _():
        pieces = []
        for shard in range(own_ref.shape[0] // 16):
            piece = own_ref[shard * 16 : shard * 16 + 16, :]
            for k, ref in zip(ORDER, came):
                part = unpacked(slot_ref, 0, shard, ref).astype(F32)
                piece = piece + jnp.where(layer_ref[0] + k < layers, part, 0.0)
            pieces.append(piece)
        total = jnp.concatenate(pieces)
        total = jnp.where(on_ref[...] > 0, total, 0.0)
        bias_ref[...] = jnp.sum(total, axis=0, keepdims=True) * (1.0 / TILE)
        pre_ref[...] = total.astype(BF)
        sums = []
        for block in [ref[packed:] for ref in (away_ref, *came)]:
            block = block.astype(F32)
            sums.append(block[0:1] + block[1:2] + block[2:3])
        loss = jnp.zeros_like(sums[0])
        for s in range(layers):
            for k in range(layers):
                mine = lax.rem(layer_ref[0] + (0, *ORDER)[k], layers) == s
                loss = loss + jnp.where(mine, sums[k], 0.0)
        loss_ref[...] = loss[:, :1] * (0.5 / count)

    grad = jnp.dot(rows_ref[...], pre_ref[...], preferred_element_type=F32)
    enc_ref[...] = (grad * (1.0 / TILE)).astype(BF)


def enc_gradient(layer, slot, rows, on, own, away, came):
    width, count = rows.shape
    feats = own.shape[1]
    whole = lambda array: pl.BlockSpec(array.shape, lambda i: (0,) * array.ndim)
    part = width // 2
    return pl.pallas_call(
        functools.partial(enc_gradient_kernel, (len(came) + 1) * count * width),
        grid=(width // part,),
        in_specs=[
            pl.BlockSpec(memory_space=pltpu.SMEM),
            pl.BlockSpec(memory_space=pltpu.SMEM),
            pl.BlockSpec((part, count), lambda i: (i, 0)),
            whole(on),
            whole(own),
            whole(away),
            *[whole(array) for array in came],
        ],
        out_specs=[
            pl.BlockSpec((part, feats), lambda i: (i, 0)),
            pl.BlockSpec((1, feats), lambda i: (0, 0)),
            pl.BlockSpec((1, 1), lambda i: (0, 0)),
        ],
        out_shape=[
            jax.ShapeDtypeStruct((width, feats), BF),
            jax.ShapeDtypeStruct((1, feats), F32),
            jax.ShapeDtypeStruct((1, 1), F32),
        ],
        scratch_shapes=[pltpu.VMEM((count, feats), BF)],
        compiler_params=params(12),
        cost_estimate=SMALL,
        name="enc_gradient",
    )(layer.reshape(1), slot, rows, on, own, away, *came)


def shards(residual, target, enc_weight, enc_bias, dec_weight, active):
    layers = dec_weight.shape[0]
    width = residual.shape[-1]
    layer = lax.axis_index("layer")
    latent = lax.axis_index("latent")
    core = latent % C

    half = spread_z(chip_rows(residual[0], core), core)
    half, target, dec, active = lax.optimization_barrier((half, target, dec_weight, active))
    rows = spread_y(half)

    chips = shard_chips(latent)
    hit = jnp.any(active == latent, axis=2)
    hit = jnp.stack(
        [
            lax.dynamic_index_in_dim(hit, (layer - k) % layers, 0, keepdims=False)
            for k in range(layers)
        ]
    )
    live = jnp.any(
        (chips[:, None] // 4 == jnp.arange(NTILE)[None, :])[None] & hit[:, None, :], axis=2
    )
    every = jnp.arange(Y * Z)
    before = every[None, :] <= every[:, None]
    slot = jnp.sum(jnp.where(before[None] & live[:, None, :], 1, 0), axis=2, dtype=jnp.int32) - 1
    slot = jnp.where(live, jnp.minimum(slot, CAP * 4 - 1), -1)
    source = jnp.sum(
        jnp.where(slot[:, None, :] == jnp.arange(CAP * 4)[None, :, None], every, 0),
        axis=2,
        dtype=jnp.int32,
    )
    source = jnp.minimum(source, Y * Z - 1)
    place = jnp.sum(
        jnp.where(chips[None, :] == every[:, None], every[None, :], 0), axis=1, dtype=jnp.int32
    )
    decoder = jnp.concatenate(
        [
            lax.dynamic_index_in_dim(dec[:, 0], (layer - k) % layers, 0, keepdims=False)
            for k in range(layers)
        ]
    )
    goal = chip_rows(target[0], core)

    packed, codes, on = encode(slot, source, enc_weight[0], enc_bias, rows)
    came = [send_layer(packed, k) for k in ORDER]
    turned, token = turn(rows, packed)
    goal, token = lax.optimization_barrier((goal, token))
    partial, sources = zip(
        *[decode(half, slot, token, codes, came, decoder) for half in range(2)]
    )
    errors = (collect(partial, core) - goal.astype(F32)).astype(BF)
    errors = spread_y(spread_z(errors, core))
    away = back(place, source, layers, decoder, errors)
    came = []
    for k, message in zip(ORDER, away):
        ring = [(s, (s - k) % layers) for s in range(layers)]
        came.append(lax.ppermute(message, "layer", ring))
    dec_grad, own = dec_gradient(layer, layers, *sources, decoder, errors)
    enc_grad, bias_grad, loss = enc_gradient(layer, slot, turned, on, own, away[0], came)
    loss = loss[0, 0]
    return (loss, enc_grad[None], bias_grad, dec_grad[:, None])


def solution(mesh):
    in_specs = (
        P("layer", "latent", None),
        P("layer", "latent", None),
        P("layer", None, "latent"),
        P("layer", "latent"),
        P(None, "layer", "latent", None),
        P(),
    )
    out_specs = (
        P(),
        P("layer", None, "latent"),
        P("layer", "latent"),
        P(None, "layer", "latent", None),
    )
    return jax.shard_map(shards, mesh=mesh, in_specs=in_specs, out_specs=out_specs, check_vma=False)
```

```python
import functools

import jax
import jax.numpy as jnp
from jax import lax
from jax.experimental import pallas as pl
from jax.experimental.pallas import tpu as pltpu
from jax.sharding import PartitionSpec as P

TILE = 64
NTILE = 8
CAP = 6
Y, Z, C = 4, 8, 2
BF = jnp.bfloat16
F32 = jnp.float32
STEPS = (0, 2, 1, 3)
ORDER = (2, 3, 1)


def index_of(y, z, c):
    return ((y % Y) * Z + z % Z) * C + c


def pairs(move, cores=(0, 1)):
    return [
        (index_of(y, z, c), index_of(*move(y, z, c)))
        for y in range(Y)
        for z in range(Z)
        for c in cores
    ]


def send(value, move, cores=(0, 1)):
    return lax.ppermute(value, "latent", pairs(move, cores))


def swap(value):
    return send(value, lambda y, z, c: (y, z, 1 - c))


def send_layer(value, steps):
    count = lax.axis_size("layer")
    return lax.ppermute(value, "layer", [(s, (s + steps) % count) for s in range(count)])


def chip_rows(value, core):
    other = swap(value)
    return jnp.where(core == 0, jnp.concatenate([value, other]), jnp.concatenate([other, value]))


def spread_z(chip, core):
    near = [
        send(chip, lambda y, z, c, k=k: (y, z ^ (k + 4 * c), c)) for k in (1, 2, 3)
    ]
    far = send(chip, lambda y, z, c: (y, z ^ 4, c), (1,))
    return jnp.concatenate([jnp.where(core == 0, chip, far)] + near)


def spread_y(half):
    parts = [half] + [send(half, lambda y, z, c, k=k: (y ^ k, z, c)) for k in STEPS[1:]]
    return parts + [swap(part) for part in parts]


def collect(halves, core):
    count, width = halves[0].shape
    pairs_of = [slice(at, at + count // 2) for at in (0, count // 2)]
    own = [
        (halves[0][at].astype(F32) + swap(halves[1][at]).astype(F32)).astype(BF)
        for at in pairs_of
    ]
    own = [part[at : at + count // Y] for part in own for at in (0, count // Y)]
    row = own[0].astype(F32)
    for part, k in zip(own[1:], STEPS[1:]):
        row = row + send(part, lambda y, z, c, k=k: (y ^ k, z, c)).astype(F32)
    row = row.astype(BF).reshape(4, 16, width)
    far = send(row[0], lambda y, z, c: (y, z ^ 4, c), (1,))
    total = jnp.where(core == 0, row[0], far).astype(F32)
    for k in (1, 2, 3):
        piece = send(row[k], lambda y, z, c, k=k: (y, z ^ (k + 4 * c), c))
        total = total + piece.astype(F32)
    total = total.astype(BF)
    return total.astype(F32) + swap(total).astype(F32)


def shard_chips(latent):
    y, z, c = latent // (Z * C), latent // C % Z, latent % C
    p = jnp.arange(Y * Z, dtype=jnp.int32)
    half, step, j = p // 16, p // 4 % 4, p % 4
    step = sum(jnp.where(step == i, to, 0) for i, to in enumerate(STEPS))
    side = (half + c) % 2
    from_z = z ^ (j + 4 * side)
    return (y ^ step) * Z + from_z


SMALL = pl.CostEstimate(flops=1000, bytes_accessed=1000, transcendentals=0)


def params(mib):
    return pltpu.CompilerParams(vmem_limit_bytes=mib * 1024 * 1024)


def join(parts, out_ref):
    at = 0
    for part in parts:
        out_ref[at : at + part.shape[0]] = part[...]
        at += part.shape[0]


def pack(source_ref, k, value_ref, out_ref):
    for place in range(CAP * TILE // 16):
        start = pl.multiple_of(source_ref[k, place] * 16, 16)
        out_ref[place * 16 : place * 16 + 16, :] = value_ref[pl.ds(start, 16), :]


def unpacked(slot_ref, k, shard, packed_ref):
    slot = slot_ref[k, shard]
    start = pl.multiple_of(lax.max(slot, 0) * 16, 16)
    value = packed_ref[pl.ds(start, 16), :]
    return jnp.where(slot >= 0, value, jnp.zeros_like(value))


def encode_kernel(slot_ref, source_ref, weight_ref, bias_ref, *refs):
    parts, (packed_ref, codes_ref, on_ref, rows_ref) = refs[:-4], refs[-4:]
    join(parts, rows_ref)
    preact = jnp.dot(rows_ref[...], weight_ref[...], preferred_element_type=F32) + bias_ref[...]
    for shard in range(Y * Z):
        at = slice(shard * 16, shard * 16 + 16)
        on = jnp.where((preact[at] > 0) & (slot_ref[0, shard] >= 0), 1.0, 0.0)
        codes_ref[at, :] = jnp.where(on > 0, preact[at], 0.0).astype(BF)
        on_ref[at, :] = on.astype(BF)
    pack(source_ref, 0, codes_ref, packed_ref)


def specs(scalars, arrays):
    return [pl.BlockSpec(memory_space=pltpu.SMEM)] * scalars + [
        pl.BlockSpec(memory_space=pltpu.VMEM)
    ] * arrays


def encode(slot, source, weight, bias, parts):
    count = sum(part.shape[0] for part in parts)
    width, feats = weight.shape
    return pl.pallas_call(
        encode_kernel,
        in_specs=specs(2, 2 + len(parts)),
        out_shape=[
            jax.ShapeDtypeStruct((CAP * TILE, feats), BF),
            jax.ShapeDtypeStruct((count, feats), BF),
            jax.ShapeDtypeStruct((count, feats), BF),
        ],
        scratch_shapes=[pltpu.VMEM((count, width), BF)],
        compiler_params=params(10),
        cost_estimate=SMALL,
        name="encode",
    )(slot, source, weight, bias, *parts)


def turn_kernel(after_ref, *refs):
    parts, (out_ref, token_ref) = refs[:-2], refs[-2:]
    at = 0
    for first, second in zip(parts[0::2], parts[1::2]):
        both = jnp.concatenate([first[...], second[...]])
        out_ref[:, at : at + both.shape[0]] = both.T
        at += both.shape[0]
    token_ref[...] = after_ref[:16, :128]


def turn(parts, after):
    count = sum(part.shape[0] for part in parts)
    return pl.pallas_call(
        turn_kernel,
        out_shape=[
            jax.ShapeDtypeStruct((parts[0].shape[1], count), BF),
            jax.ShapeDtypeStruct((16, 128), BF),
        ],
        compiler_params=params(10),
        cost_estimate=SMALL,
        name="turn",
    )(after, *parts)


def dec_gradient_kernel(layer_ref, first_ref, second_ref, weight_ref, *refs):
    del layer_ref
    parts, (out_ref, own_ref, errors_ref) = refs[:-3], refs[-3:]

    @pl.when(pl.program_id(0) == 0)
    def _():
        join(parts, errors_ref)
        own_ref[...] = lax.dot_general(
            errors_ref[...], weight_ref[...], (((1,), (1,)), ((), ())), preferred_element_type=F32
        )

    codes = jnp.concatenate([first_ref[...], second_ref[...]])
    grad = lax.dot_general(
        codes, errors_ref[...], (((0,), (0,)), ((), ())), preferred_element_type=F32
    )
    out_ref[0] = (grad * (1.0 / TILE)).astype(BF)


def dec_gradient(layer, layers, first, second, weight, parts):
    depth, width = weight.shape
    feats = depth // layers
    count = first.shape[0] + second.shape[0]
    whole = lambda array: pl.BlockSpec(array.shape, lambda k, at: (0,) * array.ndim)
    return pl.pallas_call(
        dec_gradient_kernel,
        grid_spec=pltpu.PrefetchScalarGridSpec(
            num_scalar_prefetch=1,
            grid=(layers,),
            in_specs=[
                pl.BlockSpec((first.shape[0], feats), lambda k, at: (0, k)),
                pl.BlockSpec((second.shape[0], feats), lambda k, at: (0, k)),
                pl.BlockSpec((feats, width), lambda k, at: (0, 0)),
                *[whole(part) for part in parts],
            ],
            out_specs=[
                pl.BlockSpec(
                    (1, feats, width), lambda k, at: (lax.rem(at[0] - k + layers, layers), 0, 0)
                ),
                pl.BlockSpec((count, feats), lambda k, at: (0, 0)),
            ],
            scratch_shapes=[pltpu.VMEM((count, width), BF)],
        ),
        out_shape=[
            jax.ShapeDtypeStruct((layers, feats, width), BF),
            jax.ShapeDtypeStruct((count, feats), F32),
        ],
        compiler_params=params(20),
        cost_estimate=SMALL,
        name="dec_gradient",
    )(layer.reshape(1), first, second, weight, *parts)


def add_squares(parts, out_ref, start):
    for part in parts:
        count, width = part.shape
        for at in range(0, count, 16):
            value = part[at : at + 16, :].astype(F32)
            value = value * value
            value = value[:8] + value[8:]
            total = value[:, :128]
            for lane in range(128, width, 128):
                total = total + value[:, lane : lane + 128]
            out_ref[start] = total
            start += 1


def back_kernel(layers, place_ref, source_ref, weight_ref, *refs):
    feats = weight_ref.shape[0] // layers
    away, errors_ref, back_ref, sums_ref = refs[-layers - 2 : -3], refs[-3], refs[-2], refs[-1]
    parts = refs[: -layers - 2]
    join(parts, errors_ref)
    packed = CAP * TILE
    for at, k in enumerate(ORDER):
        back_ref[at] = lax.dot_general(
            errors_ref[...],
            weight_ref[k * feats : (k + 1) * feats, :],
            (((1,), (1,)), ((), ())),
            preferred_element_type=F32,
        ).astype(BF)
        pack(source_ref, k, back_ref.at[at], away[at])
    add_squares(parts, sums_ref, 0)
    total = jnp.zeros((8, 128), F32)
    for chip in range(Y * Z):
        total = total + sums_ref[place_ref[chip]]
    left = jnp.broadcast_to(jnp.sum(total), (16, feats))
    row = lax.broadcasted_iota(jnp.int32, left.shape, 0)
    split = jnp.zeros(left.shape, F32)
    for k in range(3):
        piece = left.astype(BF).astype(F32)
        split = jnp.where(row == k, piece, split)
        left = left - piece
    for ref in away:
        ref[packed:, :] = split.astype(BF)


def back(place, source, layers, weight, parts):
    feats, width = weight.shape[0] // layers, weight.shape[1]
    count = sum(part.shape[0] for part in parts)
    return pl.pallas_call(
        functools.partial(back_kernel, layers),
        in_specs=specs(2, 1 + len(parts)),
        out_shape=[jax.ShapeDtypeStruct((CAP * TILE + 16, feats), BF)] * (layers - 1),
        scratch_shapes=[
            pltpu.VMEM((count, width), BF),
            pltpu.VMEM((layers - 1, count, feats), BF),
            pltpu.VMEM((Y * Z, 8, 128), F32),
        ],
        compiler_params=params(14),
        cost_estimate=SMALL,
        name="back",
    )(place, source, weight, *parts)


def decode_kernel(half, slot_ref, token_ref, codes_ref, weight_ref, *refs):
    del token_ref
    came, (out_ref, sources_ref) = refs[:-2], refs[-2:]
    count, feats = out_ref.shape[0], codes_ref.shape[1]
    sources_ref[:, :feats] = codes_ref[half * count : half * count + count, :]
    shards_of = count // 16
    for k, ref in zip(ORDER, came):
        for shard in range(shards_of):
            sources_ref[shard * 16 : shard * 16 + 16, k * feats : (k + 1) * feats] = unpacked(
                slot_ref, k, half * shards_of + shard, ref
            )
    out_ref[...] = jnp.dot(
        sources_ref[...], weight_ref[...], preferred_element_type=F32
    ).astype(BF)


def decode(half, slot, token, codes, came, weight):
    count = codes.shape[0] // 2
    depth, width = weight.shape
    return pl.pallas_call(
        functools.partial(decode_kernel, half),
        in_specs=specs(1, 3 + len(came)),
        out_shape=[
            jax.ShapeDtypeStruct((count, width), BF),
            jax.ShapeDtypeStruct((count, depth), BF),
        ],
        compiler_params=params(14),
        cost_estimate=SMALL,
        name="decode",
    )(slot, token, codes, weight, *came)


def enc_gradient_kernel(count, layer_ref, slot_ref, rows_ref, on_ref, own_ref, away_ref, *refs):
    came, (enc_ref, bias_ref, loss_ref, pre_ref) = refs[:-4], refs[-4:]
    packed = CAP * TILE
    layers = len(came) + 1

    @pl.when(pl.program_id(0) == 0)
    def _():
        pieces = []
        for shard in range(own_ref.shape[0] // 16):
            piece = own_ref[shard * 16 : shard * 16 + 16, :]
            for k, ref in zip(ORDER, came):
                part = unpacked(slot_ref, 0, shard, ref).astype(F32)
                piece = piece + jnp.where(layer_ref[0] + k < layers, part, 0.0)
            pieces.append(piece)
        total = jnp.concatenate(pieces)
        total = jnp.where(on_ref[...] > 0, total, 0.0)
        bias_ref[...] = jnp.sum(total, axis=0, keepdims=True) * (1.0 / TILE)
        pre_ref[...] = total.astype(BF)
        sums = []
        for block in [ref[packed:] for ref in (away_ref, *came)]:
            block = block.astype(F32)
            sums.append(block[0:1] + block[1:2] + block[2:3])
        loss = jnp.zeros_like(sums[0])
        for s in range(layers):
            for k in range(layers):
                mine = lax.rem(layer_ref[0] + (0, *ORDER)[k], layers) == s
                loss = loss + jnp.where(mine, sums[k], 0.0)
        loss_ref[...] = loss[:, :1] * (0.5 / count)

    grad = jnp.dot(rows_ref[...], pre_ref[...], preferred_element_type=F32)
    enc_ref[...] = (grad * (1.0 / TILE)).astype(BF)


def enc_gradient(layer, slot, rows, on, own, away, came):
    width, count = rows.shape
    feats = own.shape[1]
    whole = lambda array: pl.BlockSpec(array.shape, lambda i: (0,) * array.ndim)
    part = width
    return pl.pallas_call(
        functools.partial(enc_gradient_kernel, (len(came) + 1) * count * width),
        grid=(width // part,),
        in_specs=[
            pl.BlockSpec(memory_space=pltpu.SMEM),
            pl.BlockSpec(memory_space=pltpu.SMEM),
            pl.BlockSpec((part, count), lambda i: (i, 0)),
            whole(on),
            whole(own),
            whole(away),
            *[whole(array) for array in came],
        ],
        out_specs=[
            pl.BlockSpec((part, feats), lambda i: (i, 0)),
            pl.BlockSpec((1, feats), lambda i: (0, 0)),
            pl.BlockSpec((1, 1), lambda i: (0, 0)),
        ],
        out_shape=[
            jax.ShapeDtypeStruct((width, feats), BF),
            jax.ShapeDtypeStruct((1, feats), F32),
            jax.ShapeDtypeStruct((1, 1), F32),
        ],
        scratch_shapes=[pltpu.VMEM((count, feats), BF)],
        compiler_params=params(12),
        cost_estimate=SMALL,
        name="enc_gradient",
    )(layer.reshape(1), slot, rows, on, own, away, *came)


def shards(residual, target, enc_weight, enc_bias, dec_weight, active):
    layers = dec_weight.shape[0]
    width = residual.shape[-1]
    layer = lax.axis_index("layer")
    latent = lax.axis_index("latent")
    core = latent % C

    half = spread_z(chip_rows(residual[0], core), core)
    half, target, dec, active = lax.optimization_barrier((half, target, dec_weight, active))
    rows = spread_y(half)

    chips = shard_chips(latent)
    hit = jnp.any(active == latent, axis=2)
    hit = jnp.stack(
        [
            lax.dynamic_index_in_dim(hit, (layer - k) % layers, 0, keepdims=False)
            for k in range(layers)
        ]
    )
    live = jnp.any(
        (chips[:, None] // 4 == jnp.arange(NTILE)[None, :])[None] & hit[:, None, :], axis=2
    )
    every = jnp.arange(Y * Z)
    before = every[None, :] <= every[:, None]
    slot = jnp.sum(jnp.where(before[None] & live[:, None, :], 1, 0), axis=2, dtype=jnp.int32) - 1
    known = live & (layer >= jnp.arange(layers))[:, None]
    slot = jnp.where(known, jnp.minimum(slot, CAP * 4 - 1), -1)
    source = jnp.sum(
        jnp.where(slot[:, None, :] == jnp.arange(CAP * 4)[None, :, None], every, 0),
        axis=2,
        dtype=jnp.int32,
    )
    source = jnp.minimum(source, Y * Z - 1)
    place = jnp.sum(
        jnp.where(chips[None, :] == every[:, None], every[None, :], 0), axis=1, dtype=jnp.int32
    )
    decoder = jnp.concatenate(
        [
            lax.dynamic_index_in_dim(dec[:, 0], (layer - k) % layers, 0, keepdims=False)
            for k in range(layers)
        ]
    )
    goal = chip_rows(target[0], core)

    packed, codes, on = encode(slot, source, enc_weight[0], enc_bias, rows)
    came = [send_layer(packed, k) for k in ORDER]
    turned, token = turn(rows, packed)
    goal, token = lax.optimization_barrier((goal, token))
    partial, sources = zip(
        *[decode(half, slot, token, codes, came, decoder) for half in range(2)]
    )
    errors = (collect(partial, core) - goal.astype(F32)).astype(BF)
    errors = spread_y(spread_z(errors, core))
    away = back(place, source, layers, decoder, errors)
    came = [send_layer(message, -k) for k, message in zip(ORDER, away)]
    dec_grad, own = dec_gradient(layer, layers, *sources, decoder, errors)
    enc_grad, bias_grad, loss = enc_gradient(layer, slot, turned, on, own, away[0], came)
    loss = loss[0, 0]
    return (loss, enc_grad[None], bias_grad, dec_grad[:, None])


def solution(mesh):
    in_specs = (
        P("layer", "latent", None),
        P("layer", "latent", None),
        P("layer", None, "latent"),
        P("layer", "latent"),
        P(None, "layer", "latent", None),
        P(),
    )
    out_specs = (
        P(),
        P("layer", None, "latent"),
        P("layer", "latent"),
        P(None, "layer", "latent", None),
    )
    return jax.shard_map(shards, mesh=mesh, in_specs=in_specs, out_specs=out_specs, check_vma=False)
```

```python
import functools

import jax
import jax.numpy as jnp
from jax import lax
from jax.experimental import pallas as pl
from jax.experimental.pallas import tpu as pltpu
from jax.sharding import PartitionSpec as P

TILE = 64
NTILE = 8
CAP = 6
Y, Z, C = 4, 8, 2
BF = jnp.bfloat16
F32 = jnp.float32
STEPS = (0, 2, 1, 3)
ORDER = (2, 3, 1)


def index_of(y, z, c):
    return ((y % Y) * Z + z % Z) * C + c


def pairs(move, cores=(0, 1)):
    return [
        (index_of(y, z, c), index_of(*move(y, z, c)))
        for y in range(Y)
        for z in range(Z)
        for c in cores
    ]


def send(value, move, cores=(0, 1)):
    return lax.ppermute(value, "latent", pairs(move, cores))


def swap(value):
    return send(value, lambda y, z, c: (y, z, 1 - c))


def trade(value, mask):
    return lax.ppermute(value, "layer", [(s, s ^ mask) for s in range(lax.axis_size("layer"))])


def chip_rows(value, core):
    other = swap(value)
    return jnp.where(core == 0, jnp.concatenate([value, other]), jnp.concatenate([other, value]))


def spread_z(chip, core):
    near = [
        send(chip, lambda y, z, c, k=k: (y, z ^ (k + 4 * c), c)) for k in (1, 2, 3)
    ]
    far = send(chip, lambda y, z, c: (y, z ^ 4, c), (1,))
    return jnp.concatenate([jnp.where(core == 0, chip, far)] + near)


def spread_y(half):
    parts = [half] + [send(half, lambda y, z, c, k=k: (y ^ k, z, c)) for k in STEPS[1:]]
    return parts + [swap(part) for part in parts]


def collect(halves, core):
    count, width = halves[0].shape
    pairs_of = [slice(at, at + count // 2) for at in (0, count // 2)]
    own = [
        (halves[0][at].astype(F32) + swap(halves[1][at]).astype(F32)).astype(BF)
        for at in pairs_of
    ]
    own = [part[at : at + count // Y] for part in own for at in (0, count // Y)]
    row = own[0].astype(F32)
    for part, k in zip(own[1:], STEPS[1:]):
        row = row + send(part, lambda y, z, c, k=k: (y ^ k, z, c)).astype(F32)
    row = row.astype(BF).reshape(4, 16, width)
    far = send(row[0], lambda y, z, c: (y, z ^ 4, c), (1,))
    total = jnp.where(core == 0, row[0], far).astype(F32)
    for k in (1, 2, 3):
        piece = send(row[k], lambda y, z, c, k=k: (y, z ^ (k + 4 * c), c))
        total = total + piece.astype(F32)
    total = total.astype(BF)
    return total.astype(F32) + swap(total).astype(F32)


def shard_chips(latent):
    y, z, c = latent // (Z * C), latent // C % Z, latent % C
    p = jnp.arange(Y * Z, dtype=jnp.int32)
    half, step, j = p // 16, p // 4 % 4, p % 4
    step = sum(jnp.where(step == i, to, 0) for i, to in enumerate(STEPS))
    side = (half + c) % 2
    from_z = z ^ (j + 4 * side)
    return (y ^ step) * Z + from_z


SMALL = pl.CostEstimate(flops=1000, bytes_accessed=1000, transcendentals=0)


def params(mib):
    return pltpu.CompilerParams(vmem_limit_bytes=mib * 1024 * 1024)


def join(parts, out_ref):
    at = 0
    for part in parts:
        out_ref[at : at + part.shape[0]] = part[...]
        at += part.shape[0]


def pack(source_ref, k, value_ref, out_ref):
    for place in range(CAP * TILE // 16):
        start = pl.multiple_of(source_ref[k, place] * 16, 16)
        out_ref[place * 16 : place * 16 + 16, :] = value_ref[pl.ds(start, 16), :]


def unpacked(slot_ref, k, shard, packed_ref):
    slot = slot_ref[k, shard]
    start = pl.multiple_of(lax.max(slot, 0) * 16, 16)
    value = packed_ref[pl.ds(start, 16), :]
    return jnp.where(slot >= 0, value, jnp.zeros_like(value))


def encode_kernel(slot_ref, source_ref, weight_ref, bias_ref, *refs):
    parts, (packed_ref, codes_ref, on_ref, rows_ref) = refs[:-4], refs[-4:]
    join(parts, rows_ref)
    preact = jnp.dot(rows_ref[...], weight_ref[...], preferred_element_type=F32) + bias_ref[...]
    for shard in range(Y * Z):
        at = slice(shard * 16, shard * 16 + 16)
        on = jnp.where((preact[at] > 0) & (slot_ref[0, shard] >= 0), 1.0, 0.0)
        codes_ref[at, :] = jnp.where(on > 0, preact[at], 0.0).astype(BF)
        on_ref[at, :] = on.astype(BF)
    pack(source_ref, 0, codes_ref, packed_ref)


def specs(scalars, arrays):
    return [pl.BlockSpec(memory_space=pltpu.SMEM)] * scalars + [
        pl.BlockSpec(memory_space=pltpu.VMEM)
    ] * arrays


def encode(slot, source, weight, bias, parts):
    count = sum(part.shape[0] for part in parts)
    width, feats = weight.shape
    return pl.pallas_call(
        encode_kernel,
        in_specs=specs(2, 2 + len(parts)),
        out_shape=[
            jax.ShapeDtypeStruct((CAP * TILE, feats), BF),
            jax.ShapeDtypeStruct((count, feats), BF),
            jax.ShapeDtypeStruct((count, feats), BF),
        ],
        scratch_shapes=[pltpu.VMEM((count, width), BF)],
        compiler_params=params(10),
        cost_estimate=SMALL,
        name="encode",
    )(slot, source, weight, bias, *parts)


def turn_kernel(after_ref, *refs):
    parts, (out_ref, token_ref) = refs[:-2], refs[-2:]
    at = 0
    for first, second in zip(parts[0::2], parts[1::2]):
        both = jnp.concatenate([first[...], second[...]])
        out_ref[:, at : at + both.shape[0]] = both.T
        at += both.shape[0]
    token_ref[...] = after_ref[:16, :128]


def turn(parts, after):
    count = sum(part.shape[0] for part in parts)
    return pl.pallas_call(
        turn_kernel,
        out_shape=[
            jax.ShapeDtypeStruct((parts[0].shape[1], count), BF),
            jax.ShapeDtypeStruct((16, 128), BF),
        ],
        compiler_params=params(10),
        cost_estimate=SMALL,
        name="turn",
    )(after, *parts)


def dec_gradient_kernel(layer_ref, first_ref, second_ref, weight_ref, *refs):
    del layer_ref
    parts, (out_ref, own_ref, errors_ref) = refs[:-3], refs[-3:]

    @pl.when(pl.program_id(0) == 0)
    def _():
        join(parts, errors_ref)
        own_ref[...] = lax.dot_general(
            errors_ref[...], weight_ref[...], (((1,), (1,)), ((), ())), preferred_element_type=F32
        )

    codes = jnp.concatenate([first_ref[...], second_ref[...]])
    grad = lax.dot_general(
        codes, errors_ref[...], (((0,), (0,)), ((), ())), preferred_element_type=F32
    )
    out_ref[0] = (grad * (1.0 / TILE)).astype(BF)


def dec_gradient(layer, layers, first, second, weight, parts):
    depth, width = weight.shape
    feats = depth // layers
    count = first.shape[0] + second.shape[0]
    whole = lambda array: pl.BlockSpec(array.shape, lambda k, at: (0,) * array.ndim)
    return pl.pallas_call(
        dec_gradient_kernel,
        grid_spec=pltpu.PrefetchScalarGridSpec(
            num_scalar_prefetch=1,
            grid=(layers,),
            in_specs=[
                pl.BlockSpec((first.shape[0], feats), lambda k, at: (0, k)),
                pl.BlockSpec((second.shape[0], feats), lambda k, at: (0, k)),
                pl.BlockSpec((feats, width), lambda k, at: (0, 0)),
                *[whole(part) for part in parts],
            ],
            out_specs=[
                pl.BlockSpec(
                    (1, feats, width), lambda k, at: (at[0] ^ k, 0, 0)
                ),
                pl.BlockSpec((count, feats), lambda k, at: (0, 0)),
            ],
            scratch_shapes=[pltpu.VMEM((count, width), BF)],
        ),
        out_shape=[
            jax.ShapeDtypeStruct((layers, feats, width), BF),
            jax.ShapeDtypeStruct((count, feats), F32),
        ],
        compiler_params=params(20),
        cost_estimate=SMALL,
        name="dec_gradient",
    )(layer.reshape(1), first, second, weight, *parts)


def add_squares(parts, out_ref, start):
    for part in parts:
        count, width = part.shape
        for at in range(0, count, 16):
            value = part[at : at + 16, :].astype(F32)
            value = value * value
            value = value[:8] + value[8:]
            total = value[:, :128]
            for lane in range(128, width, 128):
                total = total + value[:, lane : lane + 128]
            out_ref[start] = total
            start += 1


def back_kernel(layers, place_ref, source_ref, weight_ref, *refs):
    feats = weight_ref.shape[0] // layers
    away, errors_ref, back_ref, sums_ref = refs[-layers - 2 : -3], refs[-3], refs[-2], refs[-1]
    parts = refs[: -layers - 2]
    join(parts, errors_ref)
    packed = CAP * TILE
    for at, k in enumerate(ORDER):
        back_ref[at] = lax.dot_general(
            errors_ref[...],
            weight_ref[k * feats : (k + 1) * feats, :],
            (((1,), (1,)), ((), ())),
            preferred_element_type=F32,
        ).astype(BF)
        pack(source_ref, k, back_ref.at[at], away[at])
    add_squares(parts, sums_ref, 0)
    total = jnp.zeros((8, 128), F32)
    for chip in range(Y * Z):
        total = total + sums_ref[place_ref[chip]]
    left = jnp.broadcast_to(jnp.sum(total), (16, feats))
    row = lax.broadcasted_iota(jnp.int32, left.shape, 0)
    split = jnp.zeros(left.shape, F32)
    for k in range(3):
        piece = left.astype(BF).astype(F32)
        split = jnp.where(row == k, piece, split)
        left = left - piece
    for ref in away:
        ref[packed:, :] = split.astype(BF)


def back(place, source, layers, weight, parts):
    feats, width = weight.shape[0] // layers, weight.shape[1]
    count = sum(part.shape[0] for part in parts)
    return pl.pallas_call(
        functools.partial(back_kernel, layers),
        in_specs=specs(2, 1 + len(parts)),
        out_shape=[jax.ShapeDtypeStruct((CAP * TILE + 16, feats), BF)] * (layers - 1),
        scratch_shapes=[
            pltpu.VMEM((count, width), BF),
            pltpu.VMEM((layers - 1, count, feats), BF),
            pltpu.VMEM((Y * Z, 8, 128), F32),
        ],
        compiler_params=params(14),
        cost_estimate=SMALL,
        name="back",
    )(place, source, weight, *parts)


def decode_kernel(half, slot_ref, token_ref, codes_ref, weight_ref, *refs):
    del token_ref
    came, (out_ref, sources_ref) = refs[:-2], refs[-2:]
    count, feats = out_ref.shape[0], codes_ref.shape[1]
    sources_ref[:, :feats] = codes_ref[half * count : half * count + count, :]
    shards_of = count // 16
    for k, ref in zip(ORDER, came):
        for shard in range(shards_of):
            sources_ref[shard * 16 : shard * 16 + 16, k * feats : (k + 1) * feats] = unpacked(
                slot_ref, k, half * shards_of + shard, ref
            )
    out_ref[...] = jnp.dot(
        sources_ref[...], weight_ref[...], preferred_element_type=F32
    ).astype(BF)


def decode(half, slot, token, codes, came, weight):
    count = codes.shape[0] // 2
    depth, width = weight.shape
    return pl.pallas_call(
        functools.partial(decode_kernel, half),
        in_specs=specs(1, 3 + len(came)),
        out_shape=[
            jax.ShapeDtypeStruct((count, width), BF),
            jax.ShapeDtypeStruct((count, depth), BF),
        ],
        compiler_params=params(14),
        cost_estimate=SMALL,
        name="decode",
    )(slot, token, codes, weight, *came)


def enc_gradient_kernel(count, layer_ref, slot_ref, rows_ref, on_ref, own_ref, away_ref, *refs):
    came, (enc_ref, bias_ref, loss_ref, pre_ref) = refs[:-4], refs[-4:]
    packed = CAP * TILE
    layers = len(came) + 1

    @pl.when(pl.program_id(0) == 0)
    def _():
        pieces = []
        for shard in range(own_ref.shape[0] // 16):
            piece = own_ref[shard * 16 : shard * 16 + 16, :]
            for k, ref in zip(ORDER, came):
                part = unpacked(slot_ref, 0, shard, ref).astype(F32)
                piece = piece + jnp.where((layer_ref[0] ^ k) > layer_ref[0], part, 0.0)
            pieces.append(piece)
        total = jnp.concatenate(pieces)
        total = jnp.where(on_ref[...] > 0, total, 0.0)
        bias_ref[...] = jnp.sum(total, axis=0, keepdims=True) * (1.0 / TILE)
        pre_ref[...] = total.astype(BF)
        sums = []
        for block in [ref[packed:] for ref in (away_ref, *came)]:
            block = block.astype(F32)
            sums.append(block[0:1] + block[1:2] + block[2:3])
        loss = jnp.zeros_like(sums[0])
        for s in range(layers):
            for k in range(layers):
                mine = (layer_ref[0] ^ (0, *ORDER)[k]) == s
                loss = loss + jnp.where(mine, sums[k], 0.0)
        loss_ref[...] = loss[:, :1] * (0.5 / count)

    grad = jnp.dot(rows_ref[...], pre_ref[...], preferred_element_type=F32)
    enc_ref[...] = (grad * (1.0 / TILE)).astype(BF)


def enc_gradient(layer, slot, rows, on, own, away, came):
    width, count = rows.shape
    feats = own.shape[1]
    whole = lambda array: pl.BlockSpec(array.shape, lambda i: (0,) * array.ndim)
    part = width
    return pl.pallas_call(
        functools.partial(enc_gradient_kernel, (len(came) + 1) * count * width),
        grid=(width // part,),
        in_specs=[
            pl.BlockSpec(memory_space=pltpu.SMEM),
            pl.BlockSpec(memory_space=pltpu.SMEM),
            pl.BlockSpec((part, count), lambda i: (i, 0)),
            whole(on),
            whole(own),
            whole(away),
            *[whole(array) for array in came],
        ],
        out_specs=[
            pl.BlockSpec((part, feats), lambda i: (i, 0)),
            pl.BlockSpec((1, feats), lambda i: (0, 0)),
            pl.BlockSpec((1, 1), lambda i: (0, 0)),
        ],
        out_shape=[
            jax.ShapeDtypeStruct((width, feats), BF),
            jax.ShapeDtypeStruct((1, feats), F32),
            jax.ShapeDtypeStruct((1, 1), F32),
        ],
        scratch_shapes=[pltpu.VMEM((count, feats), BF)],
        compiler_params=params(12),
        cost_estimate=SMALL,
        name="enc_gradient",
    )(layer.reshape(1), slot, rows, on, own, away, *came)


def shards(residual, target, enc_weight, enc_bias, dec_weight, active):
    layers = dec_weight.shape[0]
    width = residual.shape[-1]
    layer = lax.axis_index("layer")
    latent = lax.axis_index("latent")
    core = latent % C

    half = spread_z(chip_rows(residual[0], core), core)
    half, target, dec, active = lax.optimization_barrier((half, target, dec_weight, active))
    rows = spread_y(half)

    chips = shard_chips(latent)
    hit = jnp.any(active == latent, axis=2)
    hit = jnp.stack(
        [
            lax.dynamic_index_in_dim(hit, layer ^ k, 0, keepdims=False)
            for k in range(layers)
        ]
    )
    live = jnp.any(
        (chips[:, None] // 4 == jnp.arange(NTILE)[None, :])[None] & hit[:, None, :], axis=2
    )
    every = jnp.arange(Y * Z)
    before = every[None, :] <= every[:, None]
    slot = jnp.sum(jnp.where(before[None] & live[:, None, :], 1, 0), axis=2, dtype=jnp.int32) - 1
    known = live & (layer >= layer ^ jnp.arange(layers))[:, None]
    slot = jnp.where(known, jnp.minimum(slot, CAP * 4 - 1), -1)
    source = jnp.sum(
        jnp.where(slot[:, None, :] == jnp.arange(CAP * 4)[None, :, None], every, 0),
        axis=2,
        dtype=jnp.int32,
    )
    source = jnp.minimum(source, Y * Z - 1)
    place = jnp.sum(
        jnp.where(chips[None, :] == every[:, None], every[None, :], 0), axis=1, dtype=jnp.int32
    )
    decoder = jnp.concatenate(
        [
            lax.dynamic_index_in_dim(dec[:, 0], layer ^ k, 0, keepdims=False)
            for k in range(layers)
        ]
    )
    goal = chip_rows(target[0], core)

    packed, codes, on = encode(slot, source, enc_weight[0], enc_bias, rows)
    came = [trade(packed, k) for k in ORDER]
    turned, token = turn(rows, packed)
    goal, token = lax.optimization_barrier((goal, token))
    partial, sources = zip(
        *[decode(half, slot, token, codes, came, decoder) for half in range(2)]
    )
    errors = (collect(partial, core) - goal.astype(F32)).astype(BF)
    errors = spread_y(spread_z(errors, core))
    away = back(place, source, layers, decoder, errors)
    came = [trade(message, k) for k, message in zip(ORDER, away)]
    dec_grad, own = dec_gradient(layer, layers, *sources, decoder, errors)
    enc_grad, bias_grad, loss = enc_gradient(layer, slot, turned, on, own, away[0], came)
    loss = loss[0, 0]
    return (loss, enc_grad[None], bias_grad, dec_grad[:, None])


def solution(mesh):
    in_specs = (
        P("layer", "latent", None),
        P("layer", "latent", None),
        P("layer", None, "latent"),
        P("layer", "latent"),
        P(None, "layer", "latent", None),
        P(),
    )
    out_specs = (
        P(),
        P("layer", None, "latent"),
        P("layer", "latent"),
        P(None, "layer", "latent", None),
    )
    return jax.shard_map(shards, mesh=mesh, in_specs=in_specs, out_specs=out_specs, check_vma=False)
```
